256 devices in a mesh: dp: 32 (over y, z_hi, core), tensor: 8 (over x, z_lo).
Axes of the slice: x: 4, y: 4, z: 8 (z_hi: 4, z_lo: 2; z = z_hi * 2 + z_lo), core: 2. Of those that a mesh axis runs over, the one named last changes fastest.
Arguments:
- training_token_input: bfloat16 [8192, 8192], P('dp', 'tensor'), may hold values from -6 to 6
- gate_output_gradient: bfloat16 [8192, 29568], P('dp', 'tensor'), may hold values from -6 to 6
- up_output_gradient: bfloat16 [8192, 29568], P('dp', 'tensor'), may hold values from -6 to 6
- gate_first_matrix: bfloat16 [8192, 64], P('tensor'), may hold values from -0.0625 to 0.0625
- gate_second_matrix: bfloat16 [64, 29568], P(None, 'tensor'), may hold values from -0.75 to 0.75
- up_first_matrix: bfloat16 [8192, 64], P('tensor'), may hold values from -0.0625 to 0.0625
- up_second_matrix: bfloat16 [64, 29568], P(None, 'tensor'), may hold values from -0.75 to 0.75
- gate_weight_base: bfloat16 [8192, 29568], P('tensor', 'dp'), may hold values from -0.0625 to 0.0625
- up_weight_base: bfloat16 [8192, 29568], P('tensor', 'dp'), may hold values from -0.0625 to 0.0625
- down_weight_base: bfloat16 [29568, 8192], P('dp', 'tensor'), may hold values from -0.03125 to 0.03125
- decode_step_input: bfloat16 [2, 512, 8192], P(None, None, 'tensor'), may hold values from -6 to 6
Outputs:
- decoded: bfloat16 [2, 512, 8192], P(None, None, 'tensor')
The draws below stay inside these ranges and needn't reach their ends.
All inputs are finite; a program needn't handle non-finite values.
Results may differ from the reference program's by a relative error of at most 0.04.
Values may be sent and summed in bfloat16 or wider, within the bound.
No kernel may reach another device: no remote copies, remote signals or barrier semaphores. Data moves between devices by JAX's collectives and lax.ppermute only.
A program may use at most 64 MiB of HBM per device.

```python
import math
import jax
import jax.numpy as jnp
from jax import lax

MODEL_WIDTH = 8192
HIDDEN_UNITS = 29568
ADAPTER_RANK = 64
ROWS = 512
STEPS = 2
TOKENS = 8192
N_TENSOR = 8


def levels(own_key, shape, split, low, high):
    def one(dim, blocks):
        draws = jax.random.uniform(jax.random.fold_in(jax.random.fold_in(own_key, 6), dim), (blocks,), jnp.float32, low / len(split), high / len(split))
        return jnp.repeat(jnp.exp(draws), shape[dim] // blocks).reshape((-1,) + (1,) * (len(shape) - dim - 1))

    level = one(*split[0])
    for cut in split[1:]:
        level = level * one(*cut)
    return level


def centred(own_key, dims, scale, bound, cuts=(), kind=jnp.bfloat16):
    entries = jax.random.normal(own_key, dims, jnp.float32) * scale
    if len(cuts) > 0:
        entries = levels(own_key, dims, cuts, -0.22, 0.18) * entries
    return jnp.clip(entries, min=-bound, max=bound).astype(kind)


def setup_inputs(seed: int = 0) -> dict:
    splits = jax.random.split(jax.random.key(seed), 12)
    training_token_input = centred(splits[0], (TOKENS, MODEL_WIDTH), 1.0, 6.0, ((0, 32), (1, 8)))
    gate_output_gradient = centred(splits[1], (TOKENS, HIDDEN_UNITS), 1.0, 6.0, ((0, 32), (1, 8)))
    up_output_gradient = centred(splits[2], (TOKENS, HIDDEN_UNITS), 1.0, 6.0, ((0, 32), (1, 8)))
    gate_first_matrix = centred(splits[3], (MODEL_WIDTH, ADAPTER_RANK), MODEL_WIDTH ** -0.5, 0.0625, ((0, 8),))
    gate_second_matrix = centred(splits[4], (ADAPTER_RANK, HIDDEN_UNITS), ADAPTER_RANK ** -0.5, 0.75, ((1, 8),))
    up_first_matrix = centred(splits[5], (MODEL_WIDTH, ADAPTER_RANK), MODEL_WIDTH ** -0.5, 0.0625, ((0, 8),))
    up_second_matrix = centred(splits[6], (ADAPTER_RANK, HIDDEN_UNITS), ADAPTER_RANK ** -0.5, 0.75, ((1, 8),))
    gate_weight_base = centred(splits[7], (MODEL_WIDTH, HIDDEN_UNITS), MODEL_WIDTH ** -0.5, 0.0625, ((0, 8), (1, 32)))
    up_weight_base = centred(splits[8], (MODEL_WIDTH, HIDDEN_UNITS), MODEL_WIDTH ** -0.5, 0.0625, ((0, 8), (1, 32)))
    down_weight_base = centred(splits[9], (HIDDEN_UNITS, MODEL_WIDTH), HIDDEN_UNITS ** -0.5, 0.03125, ((0, 32), (1, 8)))
    decode_step_input = centred(splits[10], (STEPS, ROWS, MODEL_WIDTH), 1.0, 6.0, ((2, 8),))
    return {"training_token_input": training_token_input, "gate_output_gradient": gate_output_gradient, "up_output_gradient": up_output_gradient, "gate_first_matrix": gate_first_matrix, "gate_second_matrix": gate_second_matrix, "up_first_matrix": up_first_matrix, "up_second_matrix": up_second_matrix, "gate_weight_base": gate_weight_base, "up_weight_base": up_weight_base, "down_weight_base": down_weight_base, "decode_step_input": decode_step_input}


def partial_rounded(inputs, weight):
    blocks = jnp.moveaxis(inputs.reshape(inputs.shape[0], N_TENSOR, -1), 1, 0)
    pieces = weight.reshape(N_TENSOR, -1, weight.shape[1])

    def one_block(pair):
        left, right = pair
        total = jnp.dot(left, right, preferred_element_type=jnp.float32)
        return lax.optimization_barrier(total.astype(jnp.bfloat16)).astype(jnp.float32)
    terms = lax.map(one_block, (blocks, pieces))
    return lax.optimization_barrier(jnp.sum(terms, axis=0))

def reference(training_token_input, gate_output_gradient, up_output_gradient, gate_first_matrix, gate_second_matrix, up_first_matrix, up_second_matrix, gate_weight_base, up_weight_base, down_weight_base, decode_step_input):
    second_learning_rate = 0.5 / math.sqrt(ADAPTER_RANK * TOKENS)
    first_learning_rate = 0.5 / math.sqrt(MODEL_WIDTH * HIDDEN_UNITS * TOKENS / ADAPTER_RANK)

    def apply_adapter(cotangent, factor_b, factor_a, base):
        inner_b = jnp.dot(training_token_input, factor_b, preferred_element_type=jnp.float32).astype(jnp.bfloat16)
        inner_a = jnp.dot(cotangent, factor_a.T, preferred_element_type=jnp.float32).astype(jnp.bfloat16)
        grad_a = jnp.dot(inner_b.T, cotangent, preferred_element_type=jnp.float32)
        grad_b = jnp.dot(training_token_input.T, inner_a, preferred_element_type=jnp.float32)
        fresh_b = (factor_b.astype(jnp.float32) - first_learning_rate * grad_b).astype(jnp.bfloat16)
        fresh_a = (factor_a.astype(jnp.float32) - second_learning_rate * grad_a).astype(jnp.bfloat16)
        update = jnp.dot(fresh_b, fresh_a, preferred_element_type=jnp.float32)
        return (base.astype(jnp.float32) + update).astype(jnp.bfloat16)
    combined_gate_weight = apply_adapter(gate_output_gradient, gate_first_matrix, gate_second_matrix, gate_weight_base)
    combined_up_weight = apply_adapter(up_output_gradient, up_first_matrix, up_second_matrix, up_weight_base)
    results = []
    for position in range(STEPS):
        rows_in = decode_step_input[position]
        gate = partial_rounded(rows_in, combined_gate_weight)
        upper = partial_rounded(rows_in, combined_up_weight)
        hidden = (jax.nn.silu(gate) * upper).astype(jnp.bfloat16)
        results.append(jnp.dot(hidden, down_weight_base, preferred_element_type=jnp.float32).astype(jnp.bfloat16))
    return jnp.stack(results)
```

```python
import math

import jax
import jax.numpy as jnp
from jax import lax
from jax.sharding import Mesh
from jax.sharding import PartitionSpec as P

MODEL_WIDTH = 8192
HIDDEN_UNITS = 29568
ADAPTER_RANK = 64
DP = ("y", "h1", "h0", "c")
YZ = ("y", "h1", "h0")
T = ("x", "zl")
BF = jnp.bfloat16
F32 = jnp.float32


def mm(a, b):
    return jnp.dot(a, b, preferred_element_type=F32)


def everyone(value, axes):
    n = lax.axis_size(axes)
    return lax.all_to_all(jnp.broadcast_to(value[None], (n, *value.shape)), axes, 0, 0, tiled=True)


def swap_core(value):
    return lax.ppermute(value, "c", [(0, 1), (1, 0)])


def pick(pair, index):
    return lax.dynamic_index_in_dim(pair, index, 0, keepdims=False)


def reduce_tensor(tiles):
    n = lax.axis_size(T)
    me = lax.axis_index(T)
    total = pick(tiles, me).astype(F32)
    for mask in range(1, n):
        sent = pick(tiles, jnp.bitwise_xor(me, mask))
        total += lax.ppermute(sent, T, [(i, i ^ mask) for i in range(n)]).astype(F32)
    return total


def on_device(
    training_token_input,
    gate_output_gradient,
    up_output_gradient,
    gate_first_matrix,
    gate_second_matrix,
    up_first_matrix,
    up_second_matrix,
    gate_weight_base,
    up_weight_base,
    down_weight_base,
    decode_step_input,
):
    n_t = lax.axis_size(T)
    n_yz = lax.axis_size(YZ)
    core = lax.axis_index("c")
    tokens = training_token_input.shape[0]
    tokens_total = tokens * lax.axis_size(DP)
    second_rate = 0.5 / math.sqrt(ADAPTER_RANK * tokens_total)
    first_rate = 0.5 / math.sqrt(MODEL_WIDTH * HIDDEN_UNITS * tokens_total / ADAPTER_RANK)
    rank = ADAPTER_RANK
    cols = gate_weight_base.shape[1]
    steps, step_rows, feats = decode_step_input.shape
    rows = steps * step_rows
    mine = rows // n_t
    wide = 1024
    gap = wide - cols - rank

    x = decode_step_input.reshape(rows, feats)
    with jax.named_scope("inner_partials"):
        first = jnp.concatenate([gate_first_matrix, up_first_matrix], axis=1)
        inner = jnp.concatenate(
            [
                mm(training_token_input, first).astype(BF),
                mm(gate_output_gradient, gate_second_matrix.T).astype(BF),
                mm(up_output_gradient, up_second_matrix.T).astype(BF),
            ],
            axis=1,
        )
        gram = mm(x, training_token_input.T).astype(BF).reshape(n_t, mine, tokens)
    with jax.named_scope("inner_sum"):
        lines = jnp.concatenate(
            [jnp.broadcast_to(inner[None], (n_t, *inner.shape)), gram], axis=1
        )
        got = lax.all_to_all(lines, T, 0, 0, tiled=True)
    with jax.named_scope("base_product"):
        def base(weight, factor):
            left = mm(x, weight).astype(BF)
            right = mm(x, factor).astype(BF)
            return jnp.concatenate([left, jnp.zeros((rows, gap), BF), right], axis=1)

        tiles = jnp.stack(
            [
                base(gate_weight_base, gate_first_matrix).reshape(n_t, mine, wide),
                base(up_weight_base, up_first_matrix).reshape(n_t, mine, wide),
            ],
            axis=1,
        )
    got, tiles = lax.optimization_barrier((got, tiles))
    with jax.named_scope("inner_finish"):
        whole = jnp.sum(got.astype(F32), axis=0).astype(BF)
        inner_b_gate = whole[:tokens, :rank]
        inner_b_up = whole[:tokens, rank : 2 * rank]
        inner_a_gate = whole[:tokens, 2 * rank : 3 * rank]
        inner_a_up = whole[:tokens, 3 * rank :]
        gram_own = whole[tokens:]
    with jax.named_scope("grads"):
        grad = jnp.concatenate(
            [
                mm(inner_b_gate.T, gate_output_gradient).astype(BF),
                mm(inner_b_up.T, up_output_gradient).astype(BF),
            ],
            axis=0,
        )
        blocks = [grad[:, k * cols : (k + 1) * cols] for k in range(4)]
        q_part = jnp.stack([mm(gram_own, inner_a_gate), mm(gram_own, inner_a_up)]).astype(BF)

        def packed(pair):
            return jnp.concatenate([pair, jnp.zeros((2, 2 * rank, gap), BF), q_part], axis=2)

        even = packed(jnp.stack([blocks[0], blocks[2]]))
        odd = packed(jnp.stack([blocks[1], blocks[3]]))
        keep = jnp.where(core == 0, even, odd)
        send = jnp.where(core == 0, odd, even)
    with jax.named_scope("grads_core"):
        both = (keep.astype(F32) + swap_core(send).astype(F32)).astype(BF)
    with jax.named_scope("grads_yz"):
        share = 2 * rank // n_t
        chunks = both.reshape(2, n_t, share, wide).swapaxes(0, 1).reshape(n_yz, share, wide)
        arrived = lax.all_to_all(chunks, YZ, 0, 0, tiled=True)
        summed = jnp.sum(arrived.astype(F32), axis=0)
    with jax.named_scope("update_second"):
        seat = lax.axis_index(("y", "h1"))
        block = lax.axis_index(("h0", "c"))
        per = rank // share
        second = jnp.concatenate([gate_second_matrix, up_second_matrix], axis=0)
        own = lax.dynamic_slice(second, (seat * share, block * cols), (share, cols))
        new_a = (own.astype(F32) - second_rate * summed[:, :cols]).astype(BF)
        order = [
            (a * n_t + b, b * n_t + a) for a in range(n_t) for b in range(n_t)
        ]
        moved = lax.ppermute(new_a, ("y", "h1", "x", "zl"), order)
    with jax.named_scope("q_gather"):
        q_all = everyone(summed[:, wide - rank :].astype(BF), YZ)
        q_step = (
            q_all.reshape(n_t, 2, share, rank).swapaxes(0, 1).reshape(2, mine, rank).astype(F32)
        )
    with jax.named_scope("second_gather"):
        a_all = everyone(moved, T).reshape(2, rank, cols)
    with jax.named_scope("base_sum"):
        total = reduce_tensor(tiles)
    with jax.named_scope("combine"):
        q = (total[:, :, wide - rank :] - first_rate * q_step).astype(BF)
        gate = total[0, :, :cols] + mm(q[0], a_all[0])
        upper = total[1, :, :cols] + mm(q[1], a_all[1])
        hidden_own = (jax.nn.silu(gate) * upper).astype(BF)
    with jax.named_scope("hidden_gather"):
        hidden = everyone(hidden_own, T).reshape(rows, cols)
    with jax.named_scope("down"):
        out = mm(hidden, down_weight_base).astype(BF).reshape(2, rows // 2, feats)
    with jax.named_scope("out_core"):
        half = pick(out, core).astype(F32) + swap_core(pick(out, 1 - core)).astype(F32)
    with jax.named_scope("out_scatter"):
        pieces = half.astype(BF).reshape(n_yz, rows // 2 // n_yz, feats)
        landed = lax.all_to_all(pieces, YZ, 0, 0, tiled=True)
        final = jnp.sum(landed.astype(F32), axis=0).astype(BF)
    with jax.named_scope("out_gather"):
        near = everyone(final, YZ).reshape(rows // 2, feats)
        far = swap_core(near)
        low = jnp.where(core == 0, near, far)
        high = jnp.where(core == 0, far, near)
        return jnp.stack([low, high]).reshape(steps, step_rows, feats)


def solution(mesh):
    torus = Mesh(
        mesh.devices.reshape(4, 2, 2, 2, 4, 2), ("y", "h1", "h0", "c", "x", "zl")
    )
    return jax.shard_map(
        on_device,
        mesh=torus,
        in_specs=(
            P(DP, T),
            P(DP, T),
            P(DP, T),
            P(T, None),
            P(None, T),
            P(T, None),
            P(None, T),
            P(T, DP),
            P(T, DP),
            P(DP, T),
            P(None, None, T),
        ),
        out_specs=P(None, None, T),
        check_vma=False,
    )
```

```python
import math

import jax
import jax.numpy as jnp
from jax import lax
from jax.experimental import pallas as pl
from jax.experimental.pallas import tpu as pltpu
from jax.sharding import Mesh
from jax.sharding import PartitionSpec as P

MODEL_WIDTH = 8192
HIDDEN_UNITS = 29568
ADAPTER_RANK = 64
DP = ("y", "h1", "h0", "c")
YZ = ("y", "h1", "h0")
Z = ("h1", "h0")
T = ("x", "zl")
BF = jnp.bfloat16
F32 = jnp.float32


def mm(a, b):
    return jnp.dot(a, b, preferred_element_type=F32)


def everyone(value, axes):
    n = lax.axis_size(axes)
    return lax.all_to_all(jnp.broadcast_to(value[None], (n, *value.shape)), axes, 0, 0, tiled=True)


def swap_core(value):
    return lax.ppermute(value, "c", [(0, 1), (1, 0)])


def pick(pair, index):
    return lax.dynamic_index_in_dim(pair, index, 0, keepdims=False)


def nt(a, b):
    return lax.dot_general(a, b, (((1,), (1,)), ((), ())), preferred_element_type=F32)


def padded_up(n, k):
    return -(-n // k) * k


def whole_block(a):
    return pl.BlockSpec(a.shape, lambda *_: (0,) * a.ndim)


def base_kernel(x_ref, gate_ref, up_ref, gate_first_ref, up_first_ref, gate_out, up_out, stage):
    rows = x_ref[...]
    cols = gate_ref.shape[0]
    rank = gate_first_ref.shape[0]
    tall, mine = gate_out.shape[2:]
    near = gate_out.shape[0]
    stage[...] = jnp.zeros_like(stage)
    for weight, factor, out, lead in (
        (gate_ref, gate_first_ref, gate_out, True),
        (up_ref, up_first_ref, up_out, False),
    ):
        stage[:cols, :] = nt(weight[...], rows)
        stage[tall - rank :, :] = nt(factor[...], rows)
        for k in range(near):
            piece = stage[:, k * mine : (k + 1) * mine].astype(BF)
            if lead:
                out[k, 0] = piece
            else:
                out[0, k] = piece


def base_products(x, gate, up, gate_first, up_first, far, near, tall):
    rows, feats = x.shape
    mine = rows // (far * near)
    return pl.pallas_call(
        base_kernel,
        grid=(far,),
        in_specs=[
            pl.BlockSpec((mine * near, feats), lambda i: (i, 0)),
            whole_block(gate),
            whole_block(up),
            whole_block(gate_first),
            whole_block(up_first),
        ],
        out_specs=[
            pl.BlockSpec((near, 1, tall, mine), lambda i: (0, i, 0, 0)),
            pl.BlockSpec((1, near, tall, mine), lambda i: (i, 0, 0, 0)),
        ],
        out_shape=[
            jax.ShapeDtypeStruct((near, far, tall, mine), BF),
            jax.ShapeDtypeStruct((far, near, tall, mine), BF),
        ],
        scratch_shapes=[pltpu.VMEM((tall, mine * near), F32)],
        compiler_params=pltpu.CompilerParams(vmem_limit_bytes=32 * 1024 * 1024),
        cost_estimate=pl.CostEstimate(
            flops=4 * rows * feats * tall, bytes_accessed=10_000_000, transcendentals=0
        ),
    )(x, gate, up, gate_first, up_first)


def grad_kernel(core_ref, got_ref, gate_ref, up_ref, keep, send, stage):
    tokens = gate_ref.shape[1]
    ranks = tokens // 2
    rank = ranks // 2
    mine = 128
    total = got_ref[0].astype(F32)
    for t in range(1, got_ref.shape[0]):
        total += got_ref[t].astype(F32)
    total = total.astype(BF)
    first = total[:ranks]
    row = lax.broadcasted_iota(jnp.int32, first.shape, 0)
    nothing = jnp.zeros_like(first)
    gate_first = jnp.where(row < rank, first, nothing)
    up_first = jnp.where(row < rank, nothing, first)
    second = total[ranks : 2 * ranks]
    q = mm(second[:, :mine], total[2 * ranks :, :mine])
    q += mm(second[:, mine:], total[2 * ranks :, mine:])
    q = q.astype(BF)
    hidden = gate_ref.shape[0]
    step = hidden // 7
    for i in range(7):
        at = pl.ds(i * step, step)
        stage[at, :] = nt(gate_ref[at, :], gate_first) + nt(up_ref[at, :], up_first)
    stage[hidden:, :] = jnp.zeros((stage.shape[0] - hidden, ranks), F32)
    cols = hidden // 4

    def write(out, c):
        for h in range(2):
            for j in range(8):
                start = (h * 2 + c) * cols + j * mine
                out[pl.ds((j * 2 + h) * mine, mine), :] = stage[pl.ds(start, mine), :].astype(BF)
        out[16 * mine :, :] = q[c * rank : (c + 1) * rank]

    @pl.when(core_ref[0] == 0)
    def _():
        write(keep, 0)
        write(send, 1)

    @pl.when(core_ref[0] != 0)
    def _():
        write(keep, 1)
        write(send, 0)


def grads(core, got, gate, up, rank):
    hidden, tokens = gate.shape
    shape = jax.ShapeDtypeStruct((16 * 128 + rank, 128), BF)
    vmem = pl.BlockSpec(memory_space=pltpu.VMEM)
    return pl.pallas_call(
        grad_kernel,
        in_specs=[pl.BlockSpec(memory_space=pltpu.SMEM), vmem, vmem, vmem],
        out_specs=[vmem, vmem],
        out_shape=[shape, shape],
        scratch_shapes=[pltpu.VMEM((hidden + 128, 128), F32)],
        compiler_params=pltpu.CompilerParams(vmem_limit_bytes=32 * 1024 * 1024),
        cost_estimate=pl.CostEstimate(
            flops=4 * hidden * tokens * 128, bytes_accessed=6_000_000, transcendentals=0
        ),
    )(core.reshape(1), got, gate, up)


def swap_near(value):
    return lax.ppermute(value, "zl", [(0, 1), (1, 0)])


def across(value, mask):
    n = lax.axis_size("x")
    return lax.ppermute(value, "x", [(i, i ^ mask) for i in range(n)])


def on_device(
    training_token_input,
    gate_output_gradient,
    up_output_gradient,
    gate_first_matrix,
    gate_second_matrix,
    up_first_matrix,
    up_second_matrix,
    gate_weight_base,
    up_weight_base,
    down_weight_base,
    decode_step_input,
):
    n_t = lax.axis_size(T)
    n_yz = lax.axis_size(YZ)
    core = lax.axis_index("c")
    tokens = training_token_input.shape[0]
    tokens_total = tokens * lax.axis_size(DP)
    second_rate = 0.5 / math.sqrt(ADAPTER_RANK * tokens_total)
    first_rate = 0.5 / math.sqrt(MODEL_WIDTH * HIDDEN_UNITS * tokens_total / ADAPTER_RANK)
    rank = ADAPTER_RANK
    cols = gate_weight_base.shape[1]
    steps, step_rows, feats = decode_step_input.shape
    rows = steps * step_rows
    mine = rows // n_t
    tall = padded_up(cols, 16) + rank
    x_at, z_at = lax.axis_index("x"), lax.axis_index("zl")
    n_x = lax.axis_size("x")

    x = decode_step_input.reshape(rows, feats)
    gate_cot, up_cot = gate_output_gradient.T, up_output_gradient.T
    with jax.named_scope("inner_partials"):
        inner = jnp.concatenate(
            [
                nt(gate_first_matrix.T, training_token_input).astype(BF),
                nt(up_first_matrix.T, training_token_input).astype(BF),
                mm(gate_second_matrix, gate_cot).astype(BF),
                mm(up_second_matrix, up_cot).astype(BF),
            ],
            axis=0,
        )
        gram = nt(training_token_input, x).astype(BF)
        gram = gram.reshape(2, tokens // 2, n_t, mine).transpose(2, 1, 0, 3)
        gram = gram.reshape(n_t, tokens // 2, 2 * mine)
    with jax.named_scope("inner_sum"):
        lines = jnp.concatenate(
            [jnp.broadcast_to(inner[None], (n_t, *inner.shape)), gram], axis=1
        )
        got = lax.all_to_all(lines, T, 0, 0, tiled=True)
    with jax.named_scope("base_product"):
        gate_tiles, up_tiles = base_products(
            x,
            gate_weight_base.T,
            up_weight_base.T,
            gate_first_matrix.T,
            up_first_matrix.T,
            n_x,
            n_t // n_x,
            tall,
        )
        gate_send = pick(gate_tiles, 1 - z_at)
        up_sends = [pick(up_tiles, jnp.bitwise_xor(x_at, m)) for m in range(1, n_x)]
    with jax.named_scope("own_second"):
        seat = lax.axis_index(("y", "h1"))
        block = lax.axis_index(("h0", "c"))
        second = jnp.concatenate([gate_second_matrix, up_second_matrix], axis=0)
        second = jnp.pad(second.T, ((0, mine), (0, 0)))
        own = lax.dynamic_slice(second, (block * cols + seat * mine, 0), (mine, 2 * rank))
        own = own.astype(F32)
    got, gate_send, up_sends, own = lax.optimization_barrier((got, gate_send, up_sends, own))
    with jax.named_scope("base_sum_one"):
        gate_near = swap_near(gate_send)
        up_far = [across(v, m + 1) for m, v in enumerate(up_sends)]
    with jax.named_scope("grads"):
        keep, send = grads(core, got, gate_cot, up_cot, rank)
    with jax.named_scope("grads_core"):
        both = (keep.astype(F32) + swap_core(send).astype(F32)).astype(BF)
    with jax.named_scope("grads_yz"):
        chunks = jnp.concatenate(
            [
                both[: n_yz * mine].reshape(n_yz, mine, 2 * rank),
                jnp.broadcast_to(both[n_yz * mine :][None], (n_yz, rank, mine)),
            ],
            axis=1,
        )
        arrived = lax.all_to_all(chunks, YZ, 0, 0, tiled=True)
        summed = jnp.sum(arrived.astype(F32), axis=0)
    with jax.named_scope("update_second"):
        new_a = (own - second_rate * summed[:mine]).astype(BF)
        order = [
            (a * n_t + b, b * n_t + a) for a in range(n_t) for b in range(n_t)
        ]
        new_a, gate_near, up_far = lax.optimization_barrier((new_a, gate_near, up_far))
        moved = lax.ppermute(new_a, ("y", "h1", "x", "zl"), order)
    with jax.named_scope("q_other"):
        q_near = summed[mine:].astype(BF)
        q_far = swap_core(q_near)
    with jax.named_scope("base_sum_two"):
        gate_sum = (pick(gate_tiles, z_at).astype(F32) + gate_near.astype(F32)).astype(BF)
        up_sum = pick(up_tiles, x_at).astype(F32)
        for v in up_far:
            up_sum += v.astype(F32)
        up_sum = up_sum.astype(BF)
        gate_own = pick(gate_sum, x_at).astype(F32)
        for m in range(1, n_x):
            gate_own += across(pick(gate_sum, jnp.bitwise_xor(x_at, m)), m).astype(F32)
        up_own = pick(up_sum, z_at).astype(F32) + swap_near(pick(up_sum, 1 - z_at)).astype(F32)
    with jax.named_scope("second_gather"):
        a_all = everyone(moved, T).reshape(n_t * mine, 2 * rank)[:cols]
    with jax.named_scope("combine"):
        q_gate = jnp.where(core == 0, q_near, q_far).astype(F32)
        q_up = jnp.where(core == 0, q_far, q_near).astype(F32)
        q_gate = (gate_own[tall - rank :] - first_rate * q_gate).astype(BF)
        q_up = (up_own[tall - rank :] - first_rate * q_up).astype(BF)
        gate = gate_own[:cols] + mm(a_all[:, :rank], q_gate)
        upper = up_own[:cols] + mm(a_all[:, rank:], q_up)
        hidden_own = (jax.nn.silu(gate) * upper).astype(BF)
    with jax.named_scope("hidden_gather"):
        hidden = everyone(hidden_own, T)
    with jax.named_scope("down"):
        out = lax.dot_general(
            hidden, down_weight_base, (((1,), (0,)), ((), ())), preferred_element_type=F32
        )
        out = out.astype(BF).reshape(2, rows // 2, feats)
    with jax.named_scope("out_core"):
        half = pick(out, core).astype(F32) + swap_core(pick(out, 1 - core)).astype(F32)
    with jax.named_scope("out_scatter"):
        n_y, n_z = lax.axis_size("y"), lax.axis_size(Z)
        pieces = half.astype(BF).reshape(n_y, rows // 2 // n_y, feats)
        landed = lax.all_to_all(pieces, "y", 0, 0, tiled=True)
        part = jnp.sum(landed.astype(F32), axis=0).astype(BF)
        pieces = part.reshape(n_z, rows // 2 // n_y // n_z, feats)
        landed = lax.all_to_all(pieces, Z, 0, 0, tiled=True)
        final = jnp.sum(landed.astype(F32), axis=0).astype(BF)
    with jax.named_scope("out_gather"):
        line = everyone(final, Z).reshape(rows // 2 // n_y, feats)
        near = everyone(line, "y").reshape(rows // 2, feats)
        far = swap_core(near)
        low = jnp.where(core == 0, near, far)
        high = jnp.where(core == 0, far, near)
        return jnp.stack([low, high]).reshape(steps, step_rows, feats)


def solution(mesh):
    torus = Mesh(
        mesh.devices.reshape(4, 2, 2, 2, 4, 2), ("y", "h1", "h0", "c", "x", "zl")
    )
    return jax.shard_map(
        on_device,
        mesh=torus,
        in_specs=(
            P(DP, T),
            P(DP, T),
            P(DP, T),
            P(T, None),
            P(None, T),
            P(T, None),
            P(None, T),
            P(T, DP),
            P(T, DP),
            P(DP, T),
            P(None, None, T),
        ),
        out_specs=P(None, None, T),
        check_vma=False,
    )
```

```python
import math

import jax
import jax.numpy as jnp
from jax import lax
from jax.experimental import pallas as pl
from jax.experimental.pallas import tpu as pltpu
from jax.sharding import Mesh
from jax.sharding import PartitionSpec as P

MODEL_WIDTH = 8192
HIDDEN_UNITS = 29568
ADAPTER_RANK = 64
DP = ("y", "h1", "h0", "c")
YZ = ("y", "h1", "h0")
Z = ("h1", "h0")
T = ("x", "zl")
BF = jnp.bfloat16
MIB = 1024 * 1024
F32 = jnp.float32


def mm(a, b):
    return jnp.dot(a, b, preferred_element_type=F32)


def everyone(value, axes):
    n = lax.axis_size(axes)
    return lax.all_to_all(jnp.broadcast_to(value[None], (n, *value.shape)), axes, 0, 0, tiled=True)


def swap_core(value):
    return lax.ppermute(value, "c", [(0, 1), (1, 0)])


def pick(pair, index):
    return lax.dynamic_index_in_dim(pair, index, 0, keepdims=False)


def nt(a, b):
    return lax.dot_general(a, b, (((1,), (1,)), ((), ())), preferred_element_type=F32)


def padded_up(n, k):
    return -(-n // k) * k


def whole_block(a):
    return pl.BlockSpec(a.shape, lambda *_: (0,) * a.ndim)


def fetched(sources, places, sems):
    copies = [
        pltpu.make_async_copy(a, b, sems.at[k]) for k, (a, b) in enumerate(zip(sources, places))
    ]
    for copy in copies:
        copy.start()
    return copies


def base_kernel(*refs):
    sources, (gate_out, up_out, *places), (stage, sems) = refs[:5], refs[5:12], refs[12:]
    copies = fetched(sources, places, sems)
    gate_first, up_first, x, gate, up = places
    cols = gate.shape[0]
    rank = gate_first.shape[0]
    near, far, tall, mine = gate_out.shape
    pair = near * mine
    stage[...] = jnp.zeros_like(stage)
    for copy in copies[:3]:
        copy.wait()
    for weight, factor, out, copy in (
        (gate, gate_first, gate_out, copies[3]),
        (up, up_first, up_out, copies[4]),
    ):
        copy.wait()

        @pl.loop(0, far)
        def _(i):
            rows = x[pl.ds(i * pair, pair), :]
            stage[:cols, :] = nt(weight[...], rows)
            stage[tall - rank :, :] = nt(factor[...], rows)
            for k in range(near):
                piece = stage[:, k * mine : (k + 1) * mine].astype(BF)
                if out is gate_out:
                    out[k, i] = piece
                else:
                    out[i, k] = piece


def base_products(x, gate, up, gate_first, up_first, far, near, tall):
    rows, feats = x.shape
    mine = rows // (far * near)
    big = (gate_first, up_first, x, gate, up)
    return pl.pallas_call(
        base_kernel,
        in_specs=[pl.BlockSpec(memory_space=pltpu.HBM)] * len(big),
        out_specs=[pl.BlockSpec(memory_space=pltpu.VMEM)] * 2,
        out_shape=[
            jax.ShapeDtypeStruct((near, far, tall, mine), BF),
            jax.ShapeDtypeStruct((far, near, tall, mine), BF),
        ],
        scratch_shapes=[pltpu.VMEM(a.shape, BF) for a in big]
        + [pltpu.VMEM((tall, mine * near), F32), pltpu.SemaphoreType.DMA((len(big),))],
        compiler_params=pltpu.CompilerParams(vmem_limit_bytes=54 * MIB),
        cost_estimate=pl.CostEstimate(
            flops=4 * rows * feats * tall, bytes_accessed=10_000_000, transcendentals=0
        ),
    )(*big)


def inner_kernel(*refs):
    sources, (lines, gate_first, up_first, tok, x, gate_second, gate, up_second, up, sems) = (
        refs[:8],
        refs[8:],
    )
    places = (gate_first, up_first, tok, x, gate_second, gate, up_second, up)
    copies = fetched(sources, places, sems)
    n_t, height, tokens = lines.shape
    rank = gate_first.shape[0]
    mine = x.shape[0] // n_t
    ranks = 4 * rank
    for copy in copies[:3]:
        copy.wait()
    first = nt(jnp.concatenate([gate_first[...], up_first[...]], axis=0), tok[...]).astype(BF)
    for t in range(n_t):
        lines[t, : 2 * rank, :] = first
    copies[3].wait()
    for t in range(0, n_t, 2):
        gram = nt(tok[...], x[t * mine : (t + 2) * mine, :]).astype(BF)
        for k in range(2):
            for h in range(2):
                lines[t + k, ranks:, h * mine : (h + 1) * mine] = gram[
                    h * (tokens // 2) : (h + 1) * (tokens // 2), k * mine : (k + 1) * mine
                ]
    for k, (factor, cot) in enumerate(((gate_second, gate), (up_second, up))):
        copies[4 + 2 * k].wait()
        copies[5 + 2 * k].wait()
        second = mm(factor[...], cot[...]).astype(BF)
        for t in range(n_t):
            lines[t, (2 + k) * rank : (3 + k) * rank, :] = second


def inner_lines(gate_first, up_first, tok, x, gate_second, gate, up_second, up, n_t):
    tokens = tok.shape[0]
    rank = gate_first.shape[0]
    vmem = pl.BlockSpec(memory_space=pltpu.VMEM)
    big = (gate_first, up_first, tok, x, gate_second, gate, up_second, up)
    return pl.pallas_call(
        inner_kernel,
        in_specs=[pl.BlockSpec(memory_space=pltpu.HBM)] * len(big),
        out_specs=vmem,
        out_shape=jax.ShapeDtypeStruct((n_t, 4 * rank + tokens // 2, tokens), BF),
        scratch_shapes=[pltpu.VMEM(a.shape, BF) for a in big]
        + [pltpu.SemaphoreType.DMA((len(big),))],
        compiler_params=pltpu.CompilerParams(vmem_limit_bytes=56 * MIB),
        cost_estimate=pl.CostEstimate(
            flops=1_200_000_000, bytes_accessed=9_000_000, transcendentals=0
        ),
    )(*big)


def grad_kernel(core_ref, got_ref, gate_hbm, up_hbm, keep, send, stage, gate_ref, up_ref, sems):
    copies = fetched((gate_hbm, up_hbm), (gate_ref, up_ref), sems)
    tokens = gate_ref.shape[1]
    ranks = tokens // 2
    rank = ranks // 2
    mine = 128
    total = got_ref[0].astype(F32)
    for t in range(1, got_ref.shape[0]):
        total += got_ref[t].astype(F32)
    total = total.astype(BF)
    first = total[:ranks]
    row = lax.broadcasted_iota(jnp.int32, first.shape, 0)
    nothing = jnp.zeros_like(first)
    gate_first = jnp.where(row < rank, first, nothing)
    up_first = jnp.where(row < rank, nothing, first)
    second = total[ranks : 2 * ranks]
    q = mm(second[:, :mine], total[2 * ranks :, :mine])
    q += mm(second[:, mine:], total[2 * ranks :, mine:])
    q = q.astype(BF)
    hidden = gate_ref.shape[0]
    step = hidden // 7
    for copy in copies:
        copy.wait()
    for i in range(7):
        at = pl.ds(i * step, step)
        stage[at, :] = nt(gate_ref[at, :], gate_first) + nt(up_ref[at, :], up_first)
    stage[hidden:, :] = jnp.zeros((stage.shape[0] - hidden, ranks), F32)
    cols = hidden // 4

    def write(out, c):
        for h in range(2):
            for j in range(8):
                start = (h * 2 + c) * cols + j * mine
                out[pl.ds((j * 2 + h) * mine, mine), :] = stage[pl.ds(start, mine), :].astype(BF)
        out[16 * mine :, :] = q[c * rank : (c + 1) * rank]

    @pl.when(core_ref[0] == 0)
    def _():
        write(keep, 0)
        write(send, 1)

    @pl.when(core_ref[0] != 0)
    def _():
        write(keep, 1)
        write(send, 0)


def grads(core, got, gate, up, rank):
    hidden, tokens = gate.shape
    shape = jax.ShapeDtypeStruct((16 * 128 + rank, 128), BF)
    vmem = pl.BlockSpec(memory_space=pltpu.VMEM)
    return pl.pallas_call(
        grad_kernel,
        in_specs=[
            pl.BlockSpec(memory_space=pltpu.SMEM),
            vmem,
            pl.BlockSpec(memory_space=pltpu.HBM),
            pl.BlockSpec(memory_space=pltpu.HBM),
        ],
        out_specs=[vmem, vmem],
        out_shape=[shape, shape],
        scratch_shapes=[
            pltpu.VMEM((hidden + 128, 128), F32),
            pltpu.VMEM(gate.shape, BF),
            pltpu.VMEM(up.shape, BF),
            pltpu.SemaphoreType.DMA((2,)),
        ],
        compiler_params=pltpu.CompilerParams(vmem_limit_bytes=40 * MIB),
        cost_estimate=pl.CostEstimate(
            flops=4 * hidden * tokens * 128, bytes_accessed=6_000_000, transcendentals=0
        ),
    )(core.reshape(1), got, gate, up)


def swap_near(value):
    return lax.ppermute(value, "zl", [(0, 1), (1, 0)])


def across(value, mask):
    n = lax.axis_size("x")
    return lax.ppermute(value, "x", [(i, i ^ mask) for i in range(n)])


def on_device(
    training_token_input,
    gate_output_gradient,
    up_output_gradient,
    gate_first_matrix,
    gate_second_matrix,
    up_first_matrix,
    up_second_matrix,
    gate_weight_base,
    up_weight_base,
    down_weight_base,
    decode_step_input,
):
    n_t = lax.axis_size(T)
    n_yz = lax.axis_size(YZ)
    core = lax.axis_index("c")
    tokens = training_token_input.shape[0]
    tokens_total = tokens * lax.axis_size(DP)
    second_rate = 0.5 / math.sqrt(ADAPTER_RANK * tokens_total)
    first_rate = 0.5 / math.sqrt(MODEL_WIDTH * HIDDEN_UNITS * tokens_total / ADAPTER_RANK)
    rank = ADAPTER_RANK
    cols = gate_weight_base.shape[1]
    steps, step_rows, feats = decode_step_input.shape
    rows = steps * step_rows
    mine = rows // n_t
    tall = padded_up(cols, 16) + rank
    x_at, z_at = lax.axis_index("x"), lax.axis_index("zl")
    n_x = lax.axis_size("x")

    x = decode_step_input.reshape(rows, feats)
    gate_cot, up_cot = gate_output_gradient.T, up_output_gradient.T
    with jax.named_scope("inner_partials"):
        lines = inner_lines(
            gate_first_matrix.T,
            up_first_matrix.T,
            training_token_input,
            x,
            gate_second_matrix,
            gate_cot,
            up_second_matrix,
            up_cot,
            n_t,
        )
    with jax.named_scope("inner_sum"):
        got = lax.all_to_all(lines, T, 0, 0, tiled=True)
    with jax.named_scope("base_product"):
        gate_tiles, up_tiles = base_products(
            x,
            gate_weight_base.T,
            up_weight_base.T,
            gate_first_matrix.T,
            up_first_matrix.T,
            n_x,
            n_t // n_x,
            tall,
        )
        gate_send = pick(gate_tiles, 1 - z_at)
        up_sends = [pick(up_tiles, jnp.bitwise_xor(x_at, m)) for m in range(1, n_x)]
    with jax.named_scope("own_second"):
        seat = lax.axis_index(("y", "h1"))
        block = lax.axis_index(("h0", "c"))
        second = jnp.concatenate([gate_second_matrix, up_second_matrix], axis=0)
        second = jnp.pad(second, ((0, 0), (0, mine)))
        own = lax.dynamic_slice(second, (0, block * cols + seat * mine), (2 * rank, mine))
        own = own.T.astype(F32)
        got, gate_send, up_sends, own = lax.optimization_barrier(
            (got, gate_send, up_sends, own)
        )
    with jax.named_scope("base_sum_one"):
        gate_near = swap_near(gate_send)
        up_far = [across(v, m + 1) for m, v in enumerate(up_sends)]
    with jax.named_scope("grads"):
        keep, send = grads(core, got, gate_cot, up_cot, rank)
    with jax.named_scope("grads_core"):
        both = (keep.astype(F32) + swap_core(send).astype(F32)).astype(BF)
    with jax.named_scope("grads_yz"):
        n_y, n_z = lax.axis_size("y"), lax.axis_size(Z)

        def to_each(pieces, q, n):
            return jnp.concatenate(
                [pieces.reshape(n, -1, 2 * rank), jnp.broadcast_to(q[None], (n, *q.shape))], axis=1
            )

        chunks = to_each(both[: n_yz * mine], both[n_yz * mine :], n_y)
        arrived = lax.all_to_all(chunks, "y", 0, 0, tiled=True)
        summed = jnp.sum(arrived.astype(F32), axis=0).astype(BF)
        chunks = to_each(summed[: n_z * mine], summed[n_z * mine :], n_z)
        chunks, up_far[0], up_far[2] = lax.optimization_barrier((chunks, up_far[0], up_far[2]))
        arrived = lax.all_to_all(chunks, Z, 0, 0, tiled=True)
        summed = jnp.sum(arrived.astype(F32), axis=0)
    with jax.named_scope("update_second"):
        new_a = (own - second_rate * summed[:mine]).astype(BF)
        order = [
            (a * n_t + b, b * n_t + a) for a in range(n_t) for b in range(n_t)
        ]
        _, gate_near, up_far = lax.optimization_barrier((new_a, gate_near, up_far))
        moved = lax.ppermute(new_a, ("y", "h1", "x", "zl"), order)
    with jax.named_scope("q_other"):
        q_near = summed[mine:].astype(BF)
        q_far = swap_core(q_near)
    with jax.named_scope("base_sum_two"):
        gate_sum = (pick(gate_tiles, z_at).astype(F32) + gate_near.astype(F32)).astype(BF)
        up_sum = pick(up_tiles, x_at).astype(F32)
        for v in up_far:
            up_sum += v.astype(F32)
        up_sum = up_sum.astype(BF)
        gate_own = pick(gate_sum, x_at).astype(F32)
        for m in range(1, n_x):
            gate_own += across(pick(gate_sum, jnp.bitwise_xor(x_at, m)), m).astype(F32)
        up_own = pick(up_sum, z_at).astype(F32) + swap_near(pick(up_sum, 1 - z_at)).astype(F32)
    with jax.named_scope("second_gather"):
        a_all = everyone(moved, T).reshape(n_t * mine, 2 * rank)[:cols]
    with jax.named_scope("combine"):
        q_gate = jnp.where(core == 0, q_near, q_far).astype(F32)
        q_up = jnp.where(core == 0, q_far, q_near).astype(F32)
        q_gate = (gate_own[tall - rank :] - first_rate * q_gate).astype(BF)
        q_up = (up_own[tall - rank :] - first_rate * q_up).astype(BF)
        gate = gate_own[:cols] + mm(a_all[:, :rank], q_gate)
        upper = up_own[:cols] + mm(a_all[:, rank:], q_up)
        hidden_own = (jax.nn.silu(gate) * upper).astype(BF)
    with jax.named_scope("hidden_gather"):
        hidden = everyone(hidden_own, T)
    with jax.named_scope("down"):
        out = lax.dot_general(
            hidden, down_weight_base, (((1,), (0,)), ((), ())), preferred_element_type=F32
        )
        out = out.astype(BF).reshape(2, rows // 2, feats)
    with jax.named_scope("out_core"):
        half = pick(out, core).astype(F32) + swap_core(pick(out, 1 - core)).astype(F32)
    with jax.named_scope("out_scatter"):
        pieces = half.astype(BF).reshape(n_y, rows // 2 // n_y, feats)
        landed = lax.all_to_all(pieces, "y", 0, 0, tiled=True)
        part = jnp.sum(landed.astype(F32), axis=0).astype(BF)
        pieces = part.reshape(n_z, rows // 2 // n_y // n_z, feats)
        landed = lax.all_to_all(pieces, Z, 0, 0, tiled=True)
        final = jnp.sum(landed.astype(F32), axis=0).astype(BF)
    with jax.named_scope("out_gather"):
        line = everyone(final, Z).reshape(rows // 2 // n_y, feats)
        near = everyone(line, "y").reshape(rows // 2, feats)
        far = swap_core(near)
        low = jnp.where(core == 0, near, far)
        high = jnp.where(core == 0, far, near)
        return jnp.stack([low, high]).reshape(steps, step_rows, feats)


def solution(mesh):
    torus = Mesh(
        mesh.devices.reshape(4, 2, 2, 2, 4, 2), ("y", "h1", "h0", "c", "x", "zl")
    )
    return jax.shard_map(
        on_device,
        mesh=torus,
        in_specs=(
            P(DP, T),
            P(DP, T),
            P(DP, T),
            P(T, None),
            P(None, T),
            P(T, None),
            P(None, T),
            P(T, DP),
            P(T, DP),
            P(DP, T),
            P(None, None, T),
        ),
        out_specs=P(None, None, T),
        check_vma=False,
    )
```

```python
import functools
import math

import jax
import jax.numpy as jnp
from jax import lax
from jax.experimental import pallas as pl
from jax.experimental.pallas import tpu as pltpu
from jax.sharding import Mesh
from jax.sharding import PartitionSpec as P

MODEL_WIDTH = 8192
HIDDEN_UNITS = 29568
ADAPTER_RANK = 64
DP = ("y", "h1", "h0", "c")
YZ = ("y", "h1", "h0")
Z = ("h1", "h0")
T = ("x", "zl")
BF = jnp.bfloat16
MIB = 1024 * 1024
F32 = jnp.float32


def mm(a, b):
    return jnp.dot(a, b, preferred_element_type=F32)


def everyone(value, axes):
    n = lax.axis_size(axes)
    return lax.all_to_all(jnp.broadcast_to(value[None], (n, *value.shape)), axes, 0, 0, tiled=True)


def swap_core(value):
    return lax.ppermute(value, "c", [(0, 1), (1, 0)])


def pick(pair, index):
    return lax.dynamic_index_in_dim(pair, index, 0, keepdims=False)


def nt(a, b):
    return lax.dot_general(a, b, (((1,), (1,)), ((), ())), preferred_element_type=F32)


def padded_up(n, k):
    return -(-n // k) * k


def whole_block(a):
    return pl.BlockSpec(a.shape, lambda *_: (0,) * a.ndim)


def fetched(sources, places, sems):
    copies = [
        pltpu.make_async_copy(a, b, sems.at[k]) for k, (a, b) in enumerate(zip(sources, places))
    ]
    for copy in copies:
        copy.start()
    return copies


def base_kernel(*refs):
    sources, (one, two, three, *places), (stage, sems) = refs[:5], refs[5:13], refs[13:]
    copies = fetched(sources, places, sems)
    gate_first, up_first, x, gate, up = places
    cols = gate.shape[0]
    rank = gate_first.shape[0]
    near, far, mine = 2, 4, one.shape[-1]
    tall = stage.shape[0]
    rows_one, rows_two = one.shape[-2], two.shape[-2]
    low = tall - rows_one
    high = rows_two - low
    pair = near * mine
    stage[...] = jnp.zeros_like(stage)
    for copy in copies[:3]:
        copy.wait()
    for weight, factor, copy in ((gate, gate_first, copies[3]), (up, up_first, copies[4])):
        copy.wait()

        @pl.loop(0, far)
        def _(i):
            q, p = i // 2, i % 2
            at = (2 * q + jnp.bitwise_xor(p, q)) * pair
            rows = x[pl.ds(pl.multiple_of(at, pair), pair), :]
            stage[:cols, :] = nt(weight[...], rows)
            stage[tall - rank :, :] = nt(factor[...], rows)
            for k in range(near):
                lanes = slice(k * mine, (k + 1) * mine)
                if weight is gate:
                    one[p, q, k] = stage[:rows_one, lanes].astype(BF)
                    two[q, k, p, :low, :] = stage[rows_one:, lanes].astype(BF)
                else:
                    two[q, k, p, low:, :] = stage[:high, lanes].astype(BF)
                    three[k, p, q] = stage[high:, lanes].astype(BF)


def base_products(x, gate, up, gate_first, up_first, tall, parts):
    rows, feats = x.shape
    mine = rows // 8
    big = (gate_first, up_first, x, gate, up)
    return pl.pallas_call(
        base_kernel,
        in_specs=[pl.BlockSpec(memory_space=pltpu.HBM)] * len(big),
        out_specs=[pl.BlockSpec(memory_space=pltpu.VMEM)] * 3,
        out_shape=[jax.ShapeDtypeStruct((2, 2, 2, n, mine), BF) for n in parts],
        scratch_shapes=[pltpu.VMEM(a.shape, BF) for a in big]
        + [pltpu.VMEM((tall, mine * 2), F32), pltpu.SemaphoreType.DMA((len(big),))],
        compiler_params=pltpu.CompilerParams(vmem_limit_bytes=54 * MIB),
        cost_estimate=pl.CostEstimate(
            flops=4 * rows * feats * tall, bytes_accessed=10_000_000, transcendentals=0
        ),
    )(*big)


def inner_kernel(*refs):
    sources, (lines, gate_first, up_first, tok, x, gate_second, gate, up_second, up, sems) = (
        refs[:8],
        refs[8:],
    )
    places = (gate_first, up_first, tok, x, gate_second, gate, up_second, up)
    copies = fetched(sources, places, sems)
    n_t, height, tokens = lines.shape
    rank = gate_first.shape[0]
    mine = x.shape[0] // n_t
    ranks = 4 * rank
    for copy in copies[:3]:
        copy.wait()
    first = nt(jnp.concatenate([gate_first[...], up_first[...]], axis=0), tok[...]).astype(BF)
    for t in range(n_t):
        lines[t, : 2 * rank, :] = first
    copies[3].wait()
    for t in range(0, n_t, 2):
        gram = nt(tok[...], x[t * mine : (t + 2) * mine, :]).astype(BF)
        for k in range(2):
            for h in range(2):
                lines[t + k, ranks:, h * mine : (h + 1) * mine] = gram[
                    h * (tokens // 2) : (h + 1) * (tokens // 2), k * mine : (k + 1) * mine
                ]
    for k, (factor, cot) in enumerate(((gate_second, gate), (up_second, up))):
        copies[4 + 2 * k].wait()
        copies[5 + 2 * k].wait()
        second = mm(factor[...], cot[...]).astype(BF)
        for t in range(n_t):
            lines[t, (2 + k) * rank : (3 + k) * rank, :] = second


def inner_lines(gate_first, up_first, tok, x, gate_second, gate, up_second, up, n_t):
    tokens = tok.shape[0]
    rank = gate_first.shape[0]
    vmem = pl.BlockSpec(memory_space=pltpu.VMEM)
    big = (gate_first, up_first, tok, x, gate_second, gate, up_second, up)
    return pl.pallas_call(
        inner_kernel,
        in_specs=[pl.BlockSpec(memory_space=pltpu.HBM)] * len(big),
        out_specs=vmem,
        out_shape=jax.ShapeDtypeStruct((n_t, 4 * rank + tokens // 2, tokens), BF),
        scratch_shapes=[pltpu.VMEM(a.shape, BF) for a in big]
        + [pltpu.SemaphoreType.DMA((len(big),))],
        compiler_params=pltpu.CompilerParams(vmem_limit_bytes=56 * MIB),
        cost_estimate=pl.CostEstimate(
            flops=1_200_000_000, bytes_accessed=9_000_000, transcendentals=0
        ),
    )(*big)


def grad_kernel(core_ref, got_ref, gate_hbm, up_hbm, keep, send, stage, gate_ref, up_ref, sems):
    copies = fetched((gate_hbm, up_hbm), (gate_ref, up_ref), sems)
    tokens = gate_ref.shape[1]
    ranks = tokens // 2
    rank = ranks // 2
    mine = 128
    total = got_ref[0].astype(F32)
    for t in range(1, got_ref.shape[0]):
        total += got_ref[t].astype(F32)
    total = total.astype(BF)
    first = total[:ranks]
    row = lax.broadcasted_iota(jnp.int32, first.shape, 0)
    nothing = jnp.zeros_like(first)
    gate_first = jnp.where(row < rank, first, nothing)
    up_first = jnp.where(row < rank, nothing, first)
    second = total[ranks : 2 * ranks]
    q = mm(second[:, :mine], total[2 * ranks :, :mine])
    q += mm(second[:, mine:], total[2 * ranks :, mine:])
    q = q.astype(BF)
    hidden = gate_ref.shape[0]
    step = hidden // 7
    for copy in copies:
        copy.wait()
    for i in range(7):
        at = pl.ds(i * step, step)
        stage[at, :] = nt(gate_ref[at, :], gate_first) + nt(up_ref[at, :], up_first)
    stage[hidden:, :] = jnp.zeros((stage.shape[0] - hidden, ranks), F32)
    cols = hidden // 4

    def write(out, c):
        for h in range(2):
            for j in range(8):
                start = (h * 2 + c) * cols + j * mine
                out[pl.ds((j * 2 + h) * mine, mine), :] = stage[pl.ds(start, mine), :].astype(BF)
        out[16 * mine :, :] = q[c * rank : (c + 1) * rank]

    @pl.when(core_ref[0] == 0)
    def _():
        write(keep, 0)
        write(send, 1)

    @pl.when(core_ref[0] != 0)
    def _():
        write(keep, 1)
        write(send, 0)


def grads(core, got, gate, up, rank):
    hidden, tokens = gate.shape
    shape = jax.ShapeDtypeStruct((16 * 128 + rank, 128), BF)
    vmem = pl.BlockSpec(memory_space=pltpu.VMEM)
    return pl.pallas_call(
        grad_kernel,
        in_specs=[
            pl.BlockSpec(memory_space=pltpu.SMEM),
            vmem,
            pl.BlockSpec(memory_space=pltpu.HBM),
            pl.BlockSpec(memory_space=pltpu.HBM),
        ],
        out_specs=[vmem, vmem],
        out_shape=[shape, shape],
        scratch_shapes=[
            pltpu.VMEM((hidden + 128, 128), F32),
            pltpu.VMEM(gate.shape, BF),
            pltpu.VMEM(up.shape, BF),
            pltpu.SemaphoreType.DMA((2,)),
        ],
        compiler_params=pltpu.CompilerParams(vmem_limit_bytes=40 * MIB),
        cost_estimate=pl.CostEstimate(
            flops=4 * hidden * tokens * 128, bytes_accessed=6_000_000, transcendentals=0
        ),
    )(core.reshape(1), got, gate, up)


def stack_kernel(*refs):
    parts, out = refs[:-1], refs[-1]
    n, height, _ = out.shape
    pieces = [p[...] for p in parts] if parts[0].ndim == 2 else [parts[0][k] for k in range(parts[0].shape[0])]
    total = pieces[0].astype(F32)
    for piece in pieces[1:]:
        total += piece.astype(F32)
    total = total.astype(BF)
    extra = parts[0].shape[-2] - n * ((parts[0].shape[-2] - ADAPTER_RANK) // n)
    own = height - extra
    for k in range(n):
        out[k, :own, :] = total[k * own : (k + 1) * own]
        out[k, own:, :] = total[n * own :]


def summed_for_each(parts, n):
    height = (parts[0].shape[-2] - ADAPTER_RANK) // n + ADAPTER_RANK
    vmem = pl.BlockSpec(memory_space=pltpu.VMEM)
    return pl.pallas_call(
        stack_kernel,
        in_specs=[vmem] * len(parts),
        out_specs=vmem,
        out_shape=jax.ShapeDtypeStruct((n, height, parts[0].shape[-1]), BF),
        compiler_params=pltpu.CompilerParams(vmem_limit_bytes=16 * MIB),
        cost_estimate=pl.CostEstimate(flops=600_000, bytes_accessed=1_500_000, transcendentals=0),
    )(*parts)


def hidden_kernel(core_ref, one, two, three, second_ref, q_near, q_far, out, *, first_rate):
    rank, mine = q_near.shape
    cols = out.shape[1]
    tall = (one.shape[0] + two.shape[0] + three.shape[0]) // 2
    low = tall - one.shape[0]
    high = two.shape[0] - low
    even = core_ref[0] == 0
    near, far = q_near[...].astype(F32), q_far[...].astype(F32)
    q_gate = two[low - rank : low, :] - first_rate * jnp.where(even, near, far)
    q_up = three[three.shape[0] - rank :, :] - first_rate * jnp.where(even, far, near)
    nothing = jnp.zeros_like(q_gate)
    factors = jnp.concatenate(
        [
            jnp.concatenate([q_gate, nothing], axis=0),
            jnp.concatenate([nothing, q_up], axis=0),
        ],
        axis=1,
    ).astype(BF)
    ends = (0, high, one.shape[0], tall - rank)
    step = mm(second_ref[: tall - rank, :], factors)
    for start, stop in zip(ends[:-1], ends[1:]):
        if stop <= one.shape[0]:
            gate = one[start:stop, :]
        else:
            gate = two[start - one.shape[0] : stop - one.shape[0], :]
        if stop <= high:
            upper = two[low + start : low + stop, :]
        else:
            upper = three[start - high : stop - high, :]
        gate = gate + step[start:stop, :mine]
        upper = upper + step[start:stop, mine:]
        hidden = gate / (1 + jnp.exp(-gate)) * upper
        end = min(stop, cols)
        hidden = hidden[: end - start].astype(BF)
        for t in range(out.shape[0]):
            out[t, start:end, :] = hidden


def hidden_for_all(core, sums, second, q_near, q_far, cols, n, first_rate):
    vmem = pl.BlockSpec(memory_space=pltpu.VMEM)
    return pl.pallas_call(
        functools.partial(hidden_kernel, first_rate=first_rate),
        in_specs=[pl.BlockSpec(memory_space=pltpu.SMEM)] + [vmem] * 6,
        out_specs=vmem,
        out_shape=jax.ShapeDtypeStruct((n, cols, q_near.shape[1]), BF),
        compiler_params=pltpu.CompilerParams(vmem_limit_bytes=16 * MIB),
        cost_estimate=pl.CostEstimate(
            flops=60_000_000, bytes_accessed=3_500_000, transcendentals=120_000
        ),
    )(core.reshape(1), *sums, second, q_near, q_far)


def swap_near(value):
    return lax.ppermute(value, "zl", [(0, 1), (1, 0)])


def across(value, mask):
    n = lax.axis_size("x")
    return lax.ppermute(value, "x", [(i, i ^ mask) for i in range(n)])


def on_device(
    training_token_input,
    gate_output_gradient,
    up_output_gradient,
    gate_first_matrix,
    gate_second_matrix,
    up_first_matrix,
    up_second_matrix,
    gate_weight_base,
    up_weight_base,
    down_weight_base,
    decode_step_input,
):
    n_t = lax.axis_size(T)
    n_yz = lax.axis_size(YZ)
    core = lax.axis_index("c")
    tokens = training_token_input.shape[0]
    tokens_total = tokens * lax.axis_size(DP)
    second_rate = 0.5 / math.sqrt(ADAPTER_RANK * tokens_total)
    first_rate = 0.5 / math.sqrt(MODEL_WIDTH * HIDDEN_UNITS * tokens_total / ADAPTER_RANK)
    rank = ADAPTER_RANK
    cols = gate_weight_base.shape[1]
    steps, step_rows, feats = decode_step_input.shape
    rows = steps * step_rows
    mine = rows // n_t
    tall = padded_up(cols, 16) + rank
    part = padded_up(2 * tall // 3, 16)
    rest = (2 * tall - part) // 32 * 16
    parts = (part, 2 * tall - part - rest, rest)
    x_at, z_at = lax.axis_index("x"), lax.axis_index("zl")
    n_x = lax.axis_size("x")

    x = decode_step_input.reshape(rows, feats)
    gate_cot, up_cot = gate_output_gradient.T, up_output_gradient.T
    with jax.named_scope("inner_partials"):
        lines = inner_lines(
            gate_first_matrix.T,
            up_first_matrix.T,
            training_token_input,
            x,
            gate_second_matrix,
            gate_cot,
            up_second_matrix,
            up_cot,
            n_t,
        )
    with jax.named_scope("inner_sum"):
        got = lax.all_to_all(lines, T, 0, 0, tiled=True)
    with jax.named_scope("base_product"):
        tiles = base_products(
            x,
            gate_weight_base.T,
            up_weight_base.T,
            gate_first_matrix.T,
            up_first_matrix.T,
            tall,
            parts,
        )
        flips = (
            lambda v: across(v, 1),
            lambda v: across(v, 3),
            swap_near,
        )
        own_p = jnp.bitwise_and(jnp.bitwise_xor(x_at, x_at // 2), 1)
        seats = (own_p, x_at // 2, z_at)

        def kept(arrays, turn, got):
            return [
                pick(v, seats[(n + turn) % 3]).astype(F32) + g.astype(F32)
                for n, (v, g) in enumerate(zip(arrays, got))
            ]

        def sends(arrays, turn):
            return [pick(v, 1 - seats[(n + turn) % 3]) for n, v in enumerate(arrays)]

        def traded(arrays, turn):
            return [flips[(n + turn) % 3](v) for n, v in enumerate(arrays)]

        first_sends = sends(tiles, 0)
    got, first_sends = lax.optimization_barrier((got, first_sends))
    with jax.named_scope("base_sum_one"):
        first_got = traded(first_sends, 0)
    with jax.named_scope("grads"):
        keep, send = grads(core, got, gate_cot, up_cot, rank)
    with jax.named_scope("grads_core"):
        chunks = summed_for_each([keep, swap_core(send)], lax.axis_size("y"))
    with jax.named_scope("own_second"):
        seat = lax.axis_index(("y", "h1"))
        block = lax.axis_index(("h0", "c"))
        chunks, gate_second, up_second = lax.optimization_barrier(
            (chunks, gate_second_matrix, up_second_matrix)
        )
        second = jnp.concatenate([gate_second, up_second], axis=0)
        second = jnp.pad(second, ((0, 0), (0, mine)))
        own = lax.dynamic_slice(second, (0, block * cols + seat * mine), (2 * rank, mine))
        own = own.T.astype(F32)
    with jax.named_scope("grads_yz"):
        n_y, n_z = lax.axis_size("y"), lax.axis_size(Z)
        arrived = lax.all_to_all(chunks, "y", 0, 0, tiled=True)
        chunks = summed_for_each([arrived], n_z)
        chunks, first_got = lax.optimization_barrier((chunks, first_got))
        arrived = lax.all_to_all(chunks, Z, 0, 0, tiled=True)
        summed = jnp.sum(arrived.astype(F32), axis=0)
    with jax.named_scope("base_sum_two"):
        tiles = [v.astype(BF) for v in kept(tiles, 0, first_got)]
        second_got = traded(sends(tiles, 1), 1)
    with jax.named_scope("update_second"):
        new_a = (own - second_rate * summed[:mine]).astype(BF)
        order = [
            (a * n_t + b, b * n_t + a) for a in range(n_t) for b in range(n_t)
        ]
        _, second_got = lax.optimization_barrier((new_a, second_got))
        moved = lax.ppermute(new_a, ("y", "h1", "x", "zl"), order)
    with jax.named_scope("q_other"):
        q_near = summed[mine:].astype(BF)
        q_far = swap_core(q_near)
    with jax.named_scope("base_sum_three"):
        tiles = [v.astype(BF) for v in kept(tiles, 1, second_got)]
        sums = kept(tiles, 2, traded(sends(tiles, 2), 2))
    with jax.named_scope("second_gather"):
        a_all = everyone(moved, T).reshape(n_t * mine, 2 * rank)
    with jax.named_scope("combine"):
        hidden = hidden_for_all(
            core, sums, a_all, q_near, q_far, cols, n_t, first_rate
        )
    with jax.named_scope("hidden_gather"):
        hidden = lax.all_to_all(hidden, T, 0, 0, tiled=True)
    with jax.named_scope("down"):
        def down(which):
            some = lax.dynamic_slice_in_dim(hidden, which * (n_t // 2), n_t // 2, 0)
            out = lax.dot_general(
                some, down_weight_base, (((1,), (0,)), ((), ())), preferred_element_type=F32
            )
            return out.reshape(rows // 2, feats)

        other = swap_core(down(1 - core).astype(BF))
        half = down(core) + other.astype(F32)
    with jax.named_scope("out_scatter"):
        pieces = half.astype(BF).reshape(n_y, rows // 2 // n_y, feats)
        landed = lax.all_to_all(pieces, "y", 0, 0, tiled=True)
        part = jnp.sum(landed.astype(F32), axis=0).astype(BF)
        pieces = part.reshape(n_z, rows // 2 // n_y // n_z, feats)
        landed = lax.all_to_all(pieces, Z, 0, 0, tiled=True)
        final = jnp.sum(landed.astype(F32), axis=0).astype(BF)
    with jax.named_scope("out_gather"):
        line = everyone(final, Z).reshape(rows // 2 // n_y, feats)
        near = everyone(line, "y").reshape(rows // 2, feats)
        far = swap_core(near)
        low = jnp.where(core == 0, near, far)
        high = jnp.where(core == 0, far, near)
        return jnp.stack([low, high]).reshape(steps, step_rows, feats)


def solution(mesh):
    torus = Mesh(
        mesh.devices.reshape(4, 2, 2, 2, 4, 2), ("y", "h1", "h0", "c", "x", "zl")
    )
    return jax.shard_map(
        on_device,
        mesh=torus,
        in_specs=(
            P(DP, T),
            P(DP, T),
            P(DP, T),
            P(T, None),
            P(None, T),
            P(T, None),
            P(None, T),
            P(T, DP),
            P(T, DP),
            P(DP, T),
            P(None, None, T),
        ),
        out_specs=P(None, None, T),
        check_vma=False,
    )
```

```python
import functools
import math

import jax
import jax.numpy as jnp
from jax import lax
from jax.experimental import pallas as pl
from jax.experimental.pallas import tpu as pltpu
from jax.sharding import Mesh
from jax.sharding import PartitionSpec as P

MODEL_WIDTH = 8192
HIDDEN_UNITS = 29568
ADAPTER_RANK = 64
DP = ("y", "h1", "h0", "c")
YZ = ("y", "h1", "h0")
Z = ("h1", "h0")
T = ("x", "zl")
BF = jnp.bfloat16
MIB = 1024 * 1024
F32 = jnp.float32


def mm(a, b):
    return jnp.dot(a, b, preferred_element_type=F32)


def everyone(value, axes):
    n = lax.axis_size(axes)
    return lax.all_to_all(jnp.broadcast_to(value[None], (n, *value.shape)), axes, 0, 0, tiled=True)


def swap_core(value):
    return lax.ppermute(value, "c", [(0, 1), (1, 0)])


def pick(pair, index):
    return lax.dynamic_index_in_dim(pair, index, 0, keepdims=False)


def nt(a, b):
    return lax.dot_general(a, b, (((1,), (1,)), ((), ())), preferred_element_type=F32)


def padded_up(n, k):
    return -(-n // k) * k


def whole_block(a):
    return pl.BlockSpec(a.shape, lambda *_: (0,) * a.ndim)


def fetched(sources, places, sems):
    copies = [
        pltpu.make_async_copy(a, b, sems.at[k]) for k, (a, b) in enumerate(zip(sources, places))
    ]
    for copy in copies:
        copy.start()
    return copies


def base_kernel(*refs):
    sources, (one, two, three, *places), (stage, sems) = refs[:5], refs[5:13], refs[13:]
    copies = fetched(sources, places, sems)
    gate_first, up_first, x, gate, up = places
    cols = gate.shape[0]
    rank = gate_first.shape[0]
    near, far, mine = 2, 4, one.shape[-1]
    tall = stage.shape[0]
    rows_one, rows_two = one.shape[-2], two.shape[-2]
    low = tall - rows_one
    high = rows_two - low
    pair = near * mine
    stage[...] = jnp.zeros_like(stage)
    for copy in copies[:3]:
        copy.wait()
    for weight, factor, copy in ((gate, gate_first, copies[3]), (up, up_first, copies[4])):
        copy.wait()

        @pl.loop(0, far)
        def _(i):
            q, p = i // 2, i % 2
            at = (2 * q + jnp.bitwise_xor(p, q)) * pair
            rows = x[pl.ds(pl.multiple_of(at, pair), pair), :]
            stage[:cols, :] = nt(weight[...], rows)
            stage[tall - rank :, :] = nt(factor[...], rows)
            for k in range(near):
                lanes = slice(k * mine, (k + 1) * mine)
                if weight is gate:
                    one[p, q, k] = stage[:rows_one, lanes].astype(BF)
                    two[q, k, p, :low, :] = stage[rows_one:, lanes].astype(BF)
                else:
                    two[q, k, p, low:, :] = stage[:high, lanes].astype(BF)
                    three[k, p, q] = stage[high:, lanes].astype(BF)


def base_products(x, gate, up, gate_first, up_first, tall, parts):
    rows, feats = x.shape
    mine = rows // 8
    big = (gate_first, up_first, x, gate, up)
    return pl.pallas_call(
        base_kernel,
        in_specs=[pl.BlockSpec(memory_space=pltpu.HBM)] * len(big),
        out_specs=[pl.BlockSpec(memory_space=pltpu.VMEM)] * 3,
        out_shape=[jax.ShapeDtypeStruct((2, 2, 2, n, mine), BF) for n in parts],
        scratch_shapes=[pltpu.VMEM(a.shape, BF) for a in big]
        + [pltpu.VMEM((tall, mine * 2), F32), pltpu.SemaphoreType.DMA((len(big),))],
        compiler_params=pltpu.CompilerParams(vmem_limit_bytes=54 * MIB),
        cost_estimate=pl.CostEstimate(
            flops=4 * rows * feats * tall, bytes_accessed=10_000_000, transcendentals=0
        ),
    )(*big)


def inner_kernel(*refs):
    sources, (lines, gate_first, up_first, tok, x, gate_second, gate, up_second, up, sems) = (
        refs[:8],
        refs[8:],
    )
    places = (gate_first, up_first, tok, x, gate_second, gate, up_second, up)
    copies = fetched(sources, places, sems)
    n_t, height, tokens = lines.shape
    rank = gate_first.shape[0]
    mine = x.shape[0] // n_t
    ranks = 4 * rank
    for copy in copies[:3]:
        copy.wait()
    first = nt(jnp.concatenate([gate_first[...], up_first[...]], axis=0), tok[...]).astype(BF)
    for t in range(n_t):
        lines[t, : 2 * rank, :] = first
    copies[3].wait()
    for t in range(0, n_t, 2):
        gram = nt(tok[...], x[t * mine : (t + 2) * mine, :]).astype(BF)
        for k in range(2):
            for h in range(2):
                lines[t + k, ranks:, h * mine : (h + 1) * mine] = gram[
                    h * (tokens // 2) : (h + 1) * (tokens // 2), k * mine : (k + 1) * mine
                ]
    for k, (factor, cot) in enumerate(((gate_second, gate), (up_second, up))):
        copies[4 + 2 * k].wait()
        copies[5 + 2 * k].wait()
        second = mm(factor[...], cot[...]).astype(BF)
        for t in range(n_t):
            lines[t, (2 + k) * rank : (3 + k) * rank, :] = second


def inner_lines(gate_first, up_first, tok, x, gate_second, gate, up_second, up, n_t):
    tokens = tok.shape[0]
    rank = gate_first.shape[0]
    vmem = pl.BlockSpec(memory_space=pltpu.VMEM)
    big = (gate_first, up_first, tok, x, gate_second, gate, up_second, up)
    return pl.pallas_call(
        inner_kernel,
        in_specs=[pl.BlockSpec(memory_space=pltpu.HBM)] * len(big),
        out_specs=vmem,
        out_shape=jax.ShapeDtypeStruct((n_t, 4 * rank + tokens // 2, tokens), BF),
        scratch_shapes=[pltpu.VMEM(a.shape, BF) for a in big]
        + [pltpu.SemaphoreType.DMA((len(big),))],
        compiler_params=pltpu.CompilerParams(vmem_limit_bytes=56 * MIB),
        cost_estimate=pl.CostEstimate(
            flops=1_200_000_000, bytes_accessed=9_000_000, transcendentals=0
        ),
    )(*big)


def grad_kernel(core_ref, got_ref, gate_hbm, up_hbm, keep, send, stage, gate_ref, up_ref, sems):
    copies = fetched((gate_hbm, up_hbm), (gate_ref, up_ref), sems)
    tokens = gate_ref.shape[1]
    ranks = tokens // 2
    rank = ranks // 2
    mine = 128
    total = got_ref[0].astype(F32)
    for t in range(1, got_ref.shape[0]):
        total += got_ref[t].astype(F32)
    total = total.astype(BF)
    first = total[:ranks]
    row = lax.broadcasted_iota(jnp.int32, first.shape, 0)
    nothing = jnp.zeros_like(first)
    gate_first = jnp.where(row < rank, first, nothing)
    up_first = jnp.where(row < rank, nothing, first)
    second = total[ranks : 2 * ranks]
    q = mm(second[:, :mine], total[2 * ranks :, :mine])
    q += mm(second[:, mine:], total[2 * ranks :, mine:])
    q = q.astype(BF)
    hidden = gate_ref.shape[0]
    step = hidden // 7
    for copy in copies:
        copy.wait()
    for i in range(7):
        at = pl.ds(i * step, step)
        stage[at, :] = nt(gate_ref[at, :], gate_first) + nt(up_ref[at, :], up_first)
    stage[hidden:, :] = jnp.zeros((stage.shape[0] - hidden, ranks), F32)
    cols = hidden // 4

    def write(out, c):
        for h in range(2):
            for j in range(8):
                start = (h * 2 + c) * cols + j * mine
                out[pl.ds((j * 2 + h) * mine, mine), :] = stage[pl.ds(start, mine), :].astype(BF)
        out[16 * mine :, :] = q[c * rank : (c + 1) * rank]

    @pl.when(core_ref[0] == 0)
    def _():
        write(keep, 0)
        write(send, 1)

    @pl.when(core_ref[0] != 0)
    def _():
        write(keep, 1)
        write(send, 0)


def grads(core, got, gate, up, rank):
    hidden, tokens = gate.shape
    shape = jax.ShapeDtypeStruct((16 * 128 + rank, 128), BF)
    vmem = pl.BlockSpec(memory_space=pltpu.VMEM)
    return pl.pallas_call(
        grad_kernel,
        in_specs=[
            pl.BlockSpec(memory_space=pltpu.SMEM),
            vmem,
            pl.BlockSpec(memory_space=pltpu.HBM),
            pl.BlockSpec(memory_space=pltpu.HBM),
        ],
        out_specs=[vmem, vmem],
        out_shape=[shape, shape],
        scratch_shapes=[
            pltpu.VMEM((hidden + 128, 128), F32),
            pltpu.VMEM(gate.shape, BF),
            pltpu.VMEM(up.shape, BF),
            pltpu.SemaphoreType.DMA((2,)),
        ],
        compiler_params=pltpu.CompilerParams(vmem_limit_bytes=40 * MIB),
        cost_estimate=pl.CostEstimate(
            flops=4 * hidden * tokens * 128, bytes_accessed=6_000_000, transcendentals=0
        ),
    )(core.reshape(1), got, gate, up)


def stack_kernel(*refs):
    parts, out = refs[:-1], refs[-1]
    n, height, _ = out.shape
    pieces = [p[...] for p in parts] if parts[0].ndim == 2 else [parts[0][k] for k in range(parts[0].shape[0])]
    total = pieces[0].astype(F32)
    for piece in pieces[1:]:
        total += piece.astype(F32)
    total = total.astype(BF)
    extra = parts[0].shape[-2] - n * ((parts[0].shape[-2] - ADAPTER_RANK) // n)
    own = height - extra
    for k in range(n):
        out[k, :own, :] = total[k * own : (k + 1) * own]
        out[k, own:, :] = total[n * own :]


def summed_for_each(parts, n):
    height = (parts[0].shape[-2] - ADAPTER_RANK) // n + ADAPTER_RANK
    vmem = pl.BlockSpec(memory_space=pltpu.VMEM)
    return pl.pallas_call(
        stack_kernel,
        in_specs=[vmem] * len(parts),
        out_specs=vmem,
        out_shape=jax.ShapeDtypeStruct((n, height, parts[0].shape[-1]), BF),
        compiler_params=pltpu.CompilerParams(vmem_limit_bytes=16 * MIB),
        cost_estimate=pl.CostEstimate(flops=600_000, bytes_accessed=1_500_000, transcendentals=0),
    )(*parts)


def hidden_kernel(core_ref, one, two, three, second_ref, q_near, q_far, out, *, first_rate):
    rank, mine = q_near.shape
    cols = out.shape[1]
    tall = (one.shape[0] + two.shape[0] + three.shape[0]) // 2
    low = tall - one.shape[0]
    high = two.shape[0] - low
    even = core_ref[0] == 0
    near, far = q_near[...].astype(F32), q_far[...].astype(F32)
    q_gate = two[low - rank : low, :] - first_rate * jnp.where(even, near, far)
    q_up = three[three.shape[0] - rank :, :] - first_rate * jnp.where(even, far, near)
    nothing = jnp.zeros_like(q_gate)
    factors = jnp.concatenate(
        [
            jnp.concatenate([q_gate, nothing], axis=0),
            jnp.concatenate([nothing, q_up], axis=0),
        ],
        axis=1,
    ).astype(BF)
    ends = (0, high, one.shape[0], tall - rank)
    step = mm(second_ref[: tall - rank, :], factors)
    for start, stop in zip(ends[:-1], ends[1:]):
        if stop <= one.shape[0]:
            gate = one[start:stop, :]
        else:
            gate = two[start - one.shape[0] : stop - one.shape[0], :]
        if stop <= high:
            upper = two[low + start : low + stop, :]
        else:
            upper = three[start - high : stop - high, :]
        gate = gate + step[start:stop, :mine]
        upper = upper + step[start:stop, mine:]
        hidden = gate / (1 + jnp.exp(-gate)) * upper
        end = min(stop, cols)
        hidden = hidden[: end - start].astype(BF)
        for t in range(out.shape[0]):
            out[t, start:end, :] = hidden


def hidden_for_all(core, sums, second, q_near, q_far, cols, n, first_rate):
    vmem = pl.BlockSpec(memory_space=pltpu.VMEM)
    return pl.pallas_call(
        functools.partial(hidden_kernel, first_rate=first_rate),
        in_specs=[pl.BlockSpec(memory_space=pltpu.SMEM)] + [vmem] * 6,
        out_specs=vmem,
        out_shape=jax.ShapeDtypeStruct((n, cols, q_near.shape[1]), BF),
        compiler_params=pltpu.CompilerParams(vmem_limit_bytes=16 * MIB),
        cost_estimate=pl.CostEstimate(
            flops=60_000_000, bytes_accessed=3_500_000, transcendentals=120_000
        ),
    )(core.reshape(1), *sums, second, q_near, q_far)


def place_kernel(slot_ref, value, *refs):
    out, sem = refs[-2:]
    copy = pltpu.make_async_copy(value, out.at[slot_ref[0]], sem)
    copy.start()
    copy.wait()


def placed(slot, value, into=None):
    hbm = pl.BlockSpec(memory_space=pltpu.HBM)
    more = [] if into is None else [into]
    return pl.pallas_call(
        place_kernel,
        in_specs=[pl.BlockSpec(memory_space=pltpu.SMEM), pl.BlockSpec(memory_space=pltpu.VMEM)]
        + [hbm] * len(more),
        out_specs=hbm,
        out_shape=jax.ShapeDtypeStruct((2, *value.shape), value.dtype),
        scratch_shapes=[pltpu.SemaphoreType.DMA],
        input_output_aliases={} if into is None else {2: 0},
        compiler_params=pltpu.CompilerParams(vmem_limit_bytes=8 * MIB),
        cost_estimate=pl.CostEstimate(
            flops=0, bytes_accessed=4 * value.size, transcendentals=0
        ),
    )(slot.reshape(1), value, *more)


def swap_near(value):
    return lax.ppermute(value, "zl", [(0, 1), (1, 0)])


def across(value, mask):
    n = lax.axis_size("x")
    return lax.ppermute(value, "x", [(i, i ^ mask) for i in range(n)])


def on_device(
    training_token_input,
    gate_output_gradient,
    up_output_gradient,
    gate_first_matrix,
    gate_second_matrix,
    up_first_matrix,
    up_second_matrix,
    gate_weight_base,
    up_weight_base,
    down_weight_base,
    decode_step_input,
):
    n_t = lax.axis_size(T)
    n_yz = lax.axis_size(YZ)
    core = lax.axis_index("c")
    tokens = training_token_input.shape[0]
    tokens_total = tokens * lax.axis_size(DP)
    second_rate = 0.5 / math.sqrt(ADAPTER_RANK * tokens_total)
    first_rate = 0.5 / math.sqrt(MODEL_WIDTH * HIDDEN_UNITS * tokens_total / ADAPTER_RANK)
    rank = ADAPTER_RANK
    cols = gate_weight_base.shape[1]
    steps, step_rows, feats = decode_step_input.shape
    rows = steps * step_rows
    mine = rows // n_t
    tall = padded_up(cols, 16) + rank
    part = padded_up(2 * tall // 3, 16)
    rest = (2 * tall - part) // 32 * 16
    parts = (part, 2 * tall - part - rest, rest)
    x_at, z_at = lax.axis_index("x"), lax.axis_index("zl")
    n_x = lax.axis_size("x")

    x = decode_step_input.reshape(rows, feats)
    gate_cot, up_cot = gate_output_gradient.T, up_output_gradient.T
    with jax.named_scope("inner_partials"):
        lines = inner_lines(
            gate_first_matrix.T,
            up_first_matrix.T,
            training_token_input,
            x,
            gate_second_matrix,
            gate_cot,
            up_second_matrix,
            up_cot,
            n_t,
        )
    with jax.named_scope("inner_sum"):
        got = lax.all_to_all(lines, T, 0, 0, tiled=True)
    with jax.named_scope("base_product"):
        tiles = base_products(
            x,
            gate_weight_base.T,
            up_weight_base.T,
            gate_first_matrix.T,
            up_first_matrix.T,
            tall,
            parts,
        )
        flips = (
            lambda v: across(v, 1),
            lambda v: across(v, 3),
            swap_near,
        )
        own_p = jnp.bitwise_and(jnp.bitwise_xor(x_at, x_at // 2), 1)
        seats = (own_p, x_at // 2, z_at)

        def block_of(v, at):
            depth = len(at)
            start = (*at, *[0] * (v.ndim - depth))
            block = lax.dynamic_slice(v, start, (*[1] * depth, *v.shape[depth:]))
            return block.reshape(v.shape[depth:])

        def part_of(v, n, turn, last):
            return block_of(v, [seats[(n + k) % 3] for k in range(turn, last + 1)])

        def opposite(v, n, turn, last):
            at = [seats[(n + k) % 3] for k in range(turn, last)]
            return block_of(v, at + [1 - seats[(n + last) % 3]])

        def totals(levels, last, take):
            return [
                sum(take(v, n, turn, last).astype(F32) for turn, v in enumerate(values))
                for n, values in enumerate(zip(*levels))
            ]

        def sends(levels):
            return [v.astype(BF) for v in totals(levels, len(levels) - 1, opposite)]

        def traded(arrays, turn):
            return [flips[(n + turn) % 3](v) for n, v in enumerate(arrays)]

        first_sends = sends([tiles])
    got, first_sends = lax.optimization_barrier((got, first_sends))
    with jax.named_scope("base_sum_one"):
        first_got = traded(first_sends, 0)
    with jax.named_scope("grads"):
        keep, send = grads(core, got, gate_cot, up_cot, rank)
    with jax.named_scope("grads_core"):
        chunks = summed_for_each([keep, swap_core(send)], lax.axis_size("y"))
    with jax.named_scope("own_second"):
        seat = lax.axis_index(("y", "h1"))
        block = lax.axis_index(("h0", "c"))
        chunks, gate_second, up_second = lax.optimization_barrier(
            (chunks, gate_second_matrix, up_second_matrix)
        )
        second = jnp.concatenate([gate_second, up_second], axis=0)
        second = jnp.pad(second, ((0, 0), (0, mine)))
        own = lax.dynamic_slice(second, (0, block * cols + seat * mine), (2 * rank, mine))
        own = own.T.astype(F32)
    with jax.named_scope("grads_yz"):
        n_y, n_z = lax.axis_size("y"), lax.axis_size(Z)
        arrived = lax.all_to_all(chunks, "y", 0, 0, tiled=True)
        chunks = summed_for_each([arrived], n_z)
        chunks, first_got = lax.optimization_barrier((chunks, first_got))
        arrived = lax.all_to_all(chunks, Z, 0, 0, tiled=True)
        summed = jnp.sum(arrived.astype(F32), axis=0)
    with jax.named_scope("base_sum_two"):
        second_got = traded(sends([tiles, first_got]), 1)
    with jax.named_scope("update_second"):
        new_a = (own - second_rate * summed[:mine]).astype(BF)
        order = [
            (a * n_t + b, b * n_t + a) for a in range(n_t) for b in range(n_t)
        ]
        _, second_got = lax.optimization_barrier((new_a, second_got))
        moved = lax.ppermute(new_a, ("y", "h1", "x", "zl"), order)
    with jax.named_scope("q_other"):
        q_near = summed[mine:].astype(BF)
        q_far = swap_core(q_near)
    with jax.named_scope("base_sum_three"):
        third_sends = sends([tiles, first_got, second_got])
        moved, third_sends = lax.optimization_barrier((moved, third_sends))
        third_got = traded(third_sends, 2)
        sums = totals([tiles, first_got, second_got], 2, part_of)
        sums = [v + g.astype(F32) for v, g in zip(sums, third_got)]
    with jax.named_scope("second_gather"):
        a_all = everyone(moved, T).reshape(n_t * mine, 2 * rank)
    with jax.named_scope("combine"):
        hidden = hidden_for_all(
            core, sums, a_all, q_near, q_far, cols, n_t, first_rate
        )
    with jax.named_scope("hidden_gather"):
        hidden = lax.all_to_all(hidden, T, 0, 0, tiled=True)
    with jax.named_scope("down"):
        def down(which):
            some = lax.dynamic_slice_in_dim(hidden, which * (n_t // 2), n_t // 2, 0)
            out = lax.dot_general(
                some, down_weight_base, (((1,), (0,)), ((), ())), preferred_element_type=F32
            )
            return out.reshape(rows // 2, feats)

        other = swap_core(down(1 - core).astype(BF))
        half = down(core) + other.astype(F32)
    with jax.named_scope("out_scatter"):
        pieces = half.astype(BF).reshape(n_y, rows // 2 // n_y, feats)
        landed = lax.all_to_all(pieces, "y", 0, 0, tiled=True)
        part = jnp.sum(landed.astype(F32), axis=0).astype(BF)
        pieces = part.reshape(n_z, rows // 2 // n_y // n_z, feats)
        landed = lax.all_to_all(pieces, Z, 0, 0, tiled=True)
        final = jnp.sum(landed.astype(F32), axis=0).astype(BF)
    with jax.named_scope("out_gather"):
        line = everyone(final, Z).reshape(rows // 2 // n_y, feats)
        near = everyone(line, "y").reshape(rows // 2, feats)
        far = swap_core(near)
        pair = placed(1 - core, far, placed(core, near))
        return pair.reshape(steps, step_rows, feats)


def solution(mesh):
    torus = Mesh(
        mesh.devices.reshape(4, 2, 2, 2, 4, 2), ("y", "h1", "h0", "c", "x", "zl")
    )
    return jax.shard_map(
        on_device,
        mesh=torus,
        in_specs=(
            P(DP, T),
            P(DP, T),
            P(DP, T),
            P(T, None),
            P(None, T),
            P(T, None),
            P(None, T),
            P(T, DP),
            P(T, DP),
            P(DP, T),
            P(None, None, T),
        ),
        out_specs=P(None, None, T),
        check_vma=False,
    )
```

```python
import functools
import math

import jax
import jax.numpy as jnp
from jax import lax
from jax.experimental import pallas as pl
from jax.experimental.pallas import tpu as pltpu
from jax.sharding import Mesh
from jax.sharding import PartitionSpec as P

MODEL_WIDTH = 8192
HIDDEN_UNITS = 29568
ADAPTER_RANK = 64
DP = ("y", "h1", "h0", "c")
YZ = ("y", "h1", "h0")
Z = ("h1", "h0")
T = ("x", "zl")
BF = jnp.bfloat16
MIB = 1024 * 1024
F32 = jnp.float32


def mm(a, b):
    return jnp.dot(a, b, preferred_element_type=F32)


def everyone(value, axes):
    n = lax.axis_size(axes)
    return lax.all_to_all(jnp.broadcast_to(value[None], (n, *value.shape)), axes, 0, 0, tiled=True)


def swap_core(value):
    return lax.ppermute(value, "c", [(0, 1), (1, 0)])


def pick(pair, index):
    return lax.dynamic_index_in_dim(pair, index, 0, keepdims=False)


def nt(a, b):
    return lax.dot_general(a, b, (((1,), (1,)), ((), ())), preferred_element_type=F32)


def padded_up(n, k):
    return -(-n // k) * k


def whole_block(a):
    return pl.BlockSpec(a.shape, lambda *_: (0,) * a.ndim)


def fetched(sources, places, sems):
    copies = [
        pltpu.make_async_copy(a, b, sems.at[k]) for k, (a, b) in enumerate(zip(sources, places))
    ]
    for copy in copies:
        copy.start()
    return copies


def base_kernel(*refs):
    sources, (one, two, three, *places), (stage, sems) = refs[:5], refs[5:13], refs[13:]
    copies = fetched(sources, places, sems)
    gate_first, up_first, x, gate, up = places
    cols = gate.shape[0]
    rank = gate_first.shape[0]
    near, far, mine = 2, 4, one.shape[-1]
    tall = stage.shape[0]
    rows_one, rows_two = one.shape[-2], two.shape[-2]
    low = tall - rows_one
    high = rows_two - low
    pair = near * mine
    stage[...] = jnp.zeros_like(stage)
    for copy in copies[:3]:
        copy.wait()
    for weight, factor, copy in ((gate, gate_first, copies[3]), (up, up_first, copies[4])):
        copy.wait()

        @pl.loop(0, far)
        def _(i):
            q, p = i // 2, i % 2
            at = (2 * q + jnp.bitwise_xor(p, q)) * pair
            rows = x[pl.ds(pl.multiple_of(at, pair), pair), :]
            stage[:cols, :] = nt(weight[...], rows)
            stage[tall - rank :, :] = nt(factor[...], rows)
            for k in range(near):
                lanes = slice(k * mine, (k + 1) * mine)
                if weight is gate:
                    one[p, q, k] = stage[:rows_one, lanes].astype(BF)
                    two[q, k, p, :low, :] = stage[rows_one:, lanes].astype(BF)
                else:
                    two[q, k, p, low:, :] = stage[:high, lanes].astype(BF)
                    three[k, p, q] = stage[high:, lanes].astype(BF)


def base_products(x, gate, up, gate_first, up_first, tall, parts):
    rows, feats = x.shape
    mine = rows // 8
    big = (gate_first, up_first, x, gate, up)
    return pl.pallas_call(
        base_kernel,
        in_specs=[pl.BlockSpec(memory_space=pltpu.HBM)] * len(big),
        out_specs=[pl.BlockSpec(memory_space=pltpu.VMEM)] * 3,
        out_shape=[jax.ShapeDtypeStruct((2, 2, 2, n, mine), BF) for n in parts],
        scratch_shapes=[pltpu.VMEM(a.shape, BF) for a in big]
        + [pltpu.VMEM((tall, mine * 2), F32), pltpu.SemaphoreType.DMA((len(big),))],
        compiler_params=pltpu.CompilerParams(vmem_limit_bytes=54 * MIB),
        cost_estimate=pl.CostEstimate(
            flops=4 * rows * feats * tall, bytes_accessed=10_000_000, transcendentals=0
        ),
    )(*big)


def inner_kernel(*refs):
    sources, (lines, gate_first, up_first, tok, x, gate_second, gate, up_second, up, sems) = (
        refs[:8],
        refs[8:],
    )
    places = (gate_first, up_first, tok, x, gate_second, gate, up_second, up)
    copies = fetched(sources, places, sems)
    n_t, height, tokens = lines.shape
    rank = gate_first.shape[0]
    mine = x.shape[0] // n_t
    ranks = 4 * rank
    for copy in copies[:3]:
        copy.wait()
    first = nt(jnp.concatenate([gate_first[...], up_first[...]], axis=0), tok[...]).astype(BF)
    for t in range(n_t):
        lines[t, : 2 * rank, :] = first
    copies[3].wait()
    for t in range(0, n_t, 2):
        gram = nt(tok[...], x[t * mine : (t + 2) * mine, :]).astype(BF)
        for k in range(2):
            for h in range(2):
                lines[t + k, ranks:, h * mine : (h + 1) * mine] = gram[
                    h * (tokens // 2) : (h + 1) * (tokens // 2), k * mine : (k + 1) * mine
                ]
    for k, (factor, cot) in enumerate(((gate_second, gate), (up_second, up))):
        copies[4 + 2 * k].wait()
        copies[5 + 2 * k].wait()
        second = mm(factor[...], cot[...]).astype(BF)
        for t in range(n_t):
            lines[t, (2 + k) * rank : (3 + k) * rank, :] = second


def inner_lines(gate_first, up_first, tok, x, gate_second, gate, up_second, up, n_t):
    tokens = tok.shape[0]
    rank = gate_first.shape[0]
    vmem = pl.BlockSpec(memory_space=pltpu.VMEM)
    big = (gate_first, up_first, tok, x, gate_second, gate, up_second, up)
    return pl.pallas_call(
        inner_kernel,
        in_specs=[pl.BlockSpec(memory_space=pltpu.HBM)] * len(big),
        out_specs=vmem,
        out_shape=jax.ShapeDtypeStruct((n_t, 4 * rank + tokens // 2, tokens), BF),
        scratch_shapes=[pltpu.VMEM(a.shape, BF) for a in big]
        + [pltpu.SemaphoreType.DMA((len(big),))],
        compiler_params=pltpu.CompilerParams(vmem_limit_bytes=56 * MIB),
        cost_estimate=pl.CostEstimate(
            flops=1_200_000_000, bytes_accessed=9_000_000, transcendentals=0
        ),
    )(*big)


def near_kernel(*refs):
    for copy in fetched(refs[:2], refs[2:4], refs[4]):
        copy.wait()


def brought_near(one, two):
    return pl.pallas_call(
        near_kernel,
        in_specs=[pl.BlockSpec(memory_space=pltpu.HBM)] * 2,
        out_specs=[pl.BlockSpec(memory_space=pltpu.VMEM)] * 2,
        out_shape=[jax.ShapeDtypeStruct(a.shape, a.dtype) for a in (one, two)],
        scratch_shapes=[pltpu.SemaphoreType.DMA((2,))],
        compiler_params=pltpu.CompilerParams(vmem_limit_bytes=52 * MIB),
        cost_estimate=pl.CostEstimate(
            flops=0, bytes_accessed=8 * one.size, transcendentals=0
        ),
    )(one, two)


def grad_kernel(core_ref, got_ref, gate_ref, up_ref, keep, send, stage):
    tokens = gate_ref.shape[1]
    ranks = tokens // 2
    rank = ranks // 2
    mine = 128
    total = got_ref[0].astype(F32)
    for t in range(1, got_ref.shape[0]):
        total += got_ref[t].astype(F32)
    total = total.astype(BF)
    first = total[:ranks]
    row = lax.broadcasted_iota(jnp.int32, first.shape, 0)
    nothing = jnp.zeros_like(first)
    gate_first = jnp.where(row < rank, first, nothing)
    up_first = jnp.where(row < rank, nothing, first)
    second = total[ranks : 2 * ranks]
    q = mm(second[:, :mine], total[2 * ranks :, :mine])
    q += mm(second[:, mine:], total[2 * ranks :, mine:])
    q = q.astype(BF)
    hidden = gate_ref.shape[0]
    step = hidden // 7
    for i in range(7):
        at = pl.ds(i * step, step)
        stage[at, :] = nt(gate_ref[at, :], gate_first) + nt(up_ref[at, :], up_first)
    stage[hidden:, :] = jnp.zeros((stage.shape[0] - hidden, ranks), F32)
    cols = hidden // 4

    def write(out, c):
        for h in range(2):
            for j in range(8):
                start = (h * 2 + c) * cols + j * mine
                out[pl.ds((j * 2 + h) * mine, mine), :] = stage[pl.ds(start, mine), :].astype(BF)
        out[16 * mine :, :] = q[c * rank : (c + 1) * rank]

    @pl.when(core_ref[0] == 0)
    def _():
        write(keep, 0)
        write(send, 1)

    @pl.when(core_ref[0] != 0)
    def _():
        write(keep, 1)
        write(send, 0)


def grads(core, got, gate, up, rank):
    hidden, tokens = gate.shape
    shape = jax.ShapeDtypeStruct((16 * 128 + rank, 128), BF)
    vmem = pl.BlockSpec(memory_space=pltpu.VMEM)
    return pl.pallas_call(
        grad_kernel,
        in_specs=[
            pl.BlockSpec(memory_space=pltpu.SMEM),
            vmem,
            vmem,
            vmem,
        ],
        out_specs=[vmem, vmem],
        out_shape=[shape, shape],
        scratch_shapes=[
            pltpu.VMEM((hidden + 128, 128), F32),
        ],
        compiler_params=pltpu.CompilerParams(vmem_limit_bytes=16 * MIB),
        cost_estimate=pl.CostEstimate(
            flops=4 * hidden * tokens * 128, bytes_accessed=6_000_000, transcendentals=0
        ),
    )(core.reshape(1), got, gate, up)


def stack_kernel(*refs):
    parts, out = refs[:-1], refs[-1]
    n, height, _ = out.shape
    pieces = [p[...] for p in parts] if parts[0].ndim == 2 else [parts[0][k] for k in range(parts[0].shape[0])]
    total = pieces[0].astype(F32)
    for piece in pieces[1:]:
        total += piece.astype(F32)
    total = total.astype(BF)
    extra = parts[0].shape[-2] - n * ((parts[0].shape[-2] - ADAPTER_RANK) // n)
    own = height - extra
    for k in range(n):
        out[k, :own, :] = total[k * own : (k + 1) * own]
        out[k, own:, :] = total[n * own :]


def summed_for_each(parts, n):
    height = (parts[0].shape[-2] - ADAPTER_RANK) // n + ADAPTER_RANK
    vmem = pl.BlockSpec(memory_space=pltpu.VMEM)
    return pl.pallas_call(
        stack_kernel,
        in_specs=[vmem] * len(parts),
        out_specs=vmem,
        out_shape=jax.ShapeDtypeStruct((n, height, parts[0].shape[-1]), BF),
        compiler_params=pltpu.CompilerParams(vmem_limit_bytes=16 * MIB),
        cost_estimate=pl.CostEstimate(flops=600_000, bytes_accessed=1_500_000, transcendentals=0),
    )(*parts)


def hidden_kernel(core_ref, one, two, three, second_ref, q_near, q_far, out, *, first_rate):
    rank, mine = q_near.shape
    cols = out.shape[1]
    tall = (one.shape[0] + two.shape[0] + three.shape[0]) // 2
    low = tall - one.shape[0]
    high = two.shape[0] - low
    even = core_ref[0] == 0
    near, far = q_near[...].astype(F32), q_far[...].astype(F32)
    q_gate = two[low - rank : low, :] - first_rate * jnp.where(even, near, far)
    q_up = three[three.shape[0] - rank :, :] - first_rate * jnp.where(even, far, near)
    nothing = jnp.zeros_like(q_gate)
    factors = jnp.concatenate(
        [
            jnp.concatenate([q_gate, nothing], axis=0),
            jnp.concatenate([nothing, q_up], axis=0),
        ],
        axis=1,
    ).astype(BF)
    ends = (0, high, one.shape[0], tall - rank)
    step = mm(second_ref[: tall - rank, :], factors)
    for start, stop in zip(ends[:-1], ends[1:]):
        if stop <= one.shape[0]:
            gate = one[start:stop, :]
        else:
            gate = two[start - one.shape[0] : stop - one.shape[0], :]
        if stop <= high:
            upper = two[low + start : low + stop, :]
        else:
            upper = three[start - high : stop - high, :]
        gate = gate + step[start:stop, :mine]
        upper = upper + step[start:stop, mine:]
        hidden = gate / (1 + jnp.exp(-gate)) * upper
        end = min(stop, cols)
        hidden = hidden[: end - start].astype(BF)
        for t in range(out.shape[0]):
            out[t, start:end, :] = hidden


def hidden_for_all(core, sums, second, q_near, q_far, cols, n, first_rate):
    vmem = pl.BlockSpec(memory_space=pltpu.VMEM)
    return pl.pallas_call(
        functools.partial(hidden_kernel, first_rate=first_rate),
        in_specs=[pl.BlockSpec(memory_space=pltpu.SMEM)] + [vmem] * 6,
        out_specs=vmem,
        out_shape=jax.ShapeDtypeStruct((n, cols, q_near.shape[1]), BF),
        compiler_params=pltpu.CompilerParams(vmem_limit_bytes=16 * MIB),
        cost_estimate=pl.CostEstimate(
            flops=60_000_000, bytes_accessed=3_500_000, transcendentals=120_000
        ),
    )(core.reshape(1), *sums, second, q_near, q_far)


def place_kernel(slot_ref, value, *refs):
    out, sem = refs[-2:]
    copy = pltpu.make_async_copy(value, out.at[slot_ref[0]], sem)
    copy.start()
    copy.wait()


def placed(slot, value, into=None):
    hbm = pl.BlockSpec(memory_space=pltpu.HBM)
    more = [] if into is None else [into]
    return pl.pallas_call(
        place_kernel,
        in_specs=[pl.BlockSpec(memory_space=pltpu.SMEM), pl.BlockSpec(memory_space=pltpu.VMEM)]
        + [hbm] * len(more),
        out_specs=hbm,
        out_shape=jax.ShapeDtypeStruct((2, *value.shape), value.dtype),
        scratch_shapes=[pltpu.SemaphoreType.DMA],
        input_output_aliases={} if into is None else {2: 0},
        compiler_params=pltpu.CompilerParams(vmem_limit_bytes=8 * MIB),
        cost_estimate=pl.CostEstimate(
            flops=0, bytes_accessed=4 * value.size, transcendentals=0
        ),
    )(slot.reshape(1), value, *more)


def swap_near(value):
    return lax.ppermute(value, "zl", [(0, 1), (1, 0)])


def across(value, mask):
    n = lax.axis_size("x")
    return lax.ppermute(value, "x", [(i, i ^ mask) for i in range(n)])


def on_device(
    training_token_input,
    gate_output_gradient,
    up_output_gradient,
    gate_first_matrix,
    gate_second_matrix,
    up_first_matrix,
    up_second_matrix,
    gate_weight_base,
    up_weight_base,
    down_weight_base,
    decode_step_input,
):
    n_t = lax.axis_size(T)
    n_yz = lax.axis_size(YZ)
    core = lax.axis_index("c")
    tokens = training_token_input.shape[0]
    tokens_total = tokens * lax.axis_size(DP)
    second_rate = 0.5 / math.sqrt(ADAPTER_RANK * tokens_total)
    first_rate = 0.5 / math.sqrt(MODEL_WIDTH * HIDDEN_UNITS * tokens_total / ADAPTER_RANK)
    rank = ADAPTER_RANK
    cols = gate_weight_base.shape[1]
    steps, step_rows, feats = decode_step_input.shape
    rows = steps * step_rows
    mine = rows // n_t
    tall = padded_up(cols, 16) + rank
    part = padded_up(2 * tall // 3, 16)
    rest = (2 * tall - part) // 32 * 16
    parts = (part, 2 * tall - part - rest, rest)
    x_at, z_at = lax.axis_index("x"), lax.axis_index("zl")
    n_x = lax.axis_size("x")

    x = decode_step_input.reshape(rows, feats)
    gate_cot, up_cot = gate_output_gradient.T, up_output_gradient.T
    with jax.named_scope("inner_partials"):
        lines = inner_lines(
            gate_first_matrix.T,
            up_first_matrix.T,
            training_token_input,
            x,
            gate_second_matrix,
            gate_cot,
            up_second_matrix,
            up_cot,
            n_t,
        )
    with jax.named_scope("inner_sum"):
        got = lax.all_to_all(lines, T, 0, 0, tiled=True)
    with jax.named_scope("base_product"):
        tiles = base_products(
            x,
            gate_weight_base.T,
            up_weight_base.T,
            gate_first_matrix.T,
            up_first_matrix.T,
            tall,
            parts,
        )
        flips = (
            lambda v: across(v, 1),
            lambda v: across(v, 3),
            swap_near,
        )
        own_p = jnp.bitwise_and(jnp.bitwise_xor(x_at, x_at // 2), 1)
        seats = (own_p, x_at // 2, z_at)

        def block_of(v, at):
            depth = len(at)
            start = (*at, *[0] * (v.ndim - depth))
            block = lax.dynamic_slice(v, start, (*[1] * depth, *v.shape[depth:]))
            return block.reshape(v.shape[depth:])

        def part_of(v, n, turn, last):
            return block_of(v, [seats[(n + k) % 3] for k in range(turn, last + 1)])

        def opposite(v, n, turn, last):
            at = [seats[(n + k) % 3] for k in range(turn, last)]
            return block_of(v, at + [1 - seats[(n + last) % 3]])

        def totals(levels, last, take):
            return [
                sum(take(v, n, turn, last).astype(F32) for turn, v in enumerate(values))
                for n, values in enumerate(zip(*levels))
            ]

        def sends(levels):
            return [v.astype(BF) for v in totals(levels, len(levels) - 1, opposite)]

        def traded(arrays, turn):
            return [flips[(n + turn) % 3](v) for n, v in enumerate(arrays)]

        first_sends = sends([tiles])
    got, first_sends = lax.optimization_barrier((got, first_sends))
    with jax.named_scope("base_sum_one"):
        first_got = traded(first_sends, 0)
    with jax.named_scope("grads"):
        got, gate_cot, up_cot = lax.optimization_barrier((got, gate_cot, up_cot))
        keep, send = grads(core, got, *brought_near(gate_cot, up_cot), rank)
    with jax.named_scope("grads_core"):
        chunks = summed_for_each([keep, swap_core(send)], lax.axis_size("y"))
    with jax.named_scope("own_second"):
        seat = lax.axis_index(("y", "h1"))
        block = lax.axis_index(("h0", "c"))
        chunks, gate_second, up_second = lax.optimization_barrier(
            (chunks, gate_second_matrix, up_second_matrix)
        )
        second = jnp.concatenate([gate_second, up_second], axis=0)
        second = jnp.pad(second, ((0, 0), (0, mine)))
        own = lax.dynamic_slice(second, (0, block * cols + seat * mine), (2 * rank, mine))
        own = own.T.astype(F32)
    with jax.named_scope("grads_yz"):
        n_y, n_z = lax.axis_size("y"), lax.axis_size(Z)
        arrived = lax.all_to_all(chunks, "y", 0, 0, tiled=True)
        chunks = summed_for_each([arrived], n_z)
        chunks, first_got = lax.optimization_barrier((chunks, first_got))
        arrived = lax.all_to_all(chunks, Z, 0, 0, tiled=True)
        summed = jnp.sum(arrived.astype(F32), axis=0)
    with jax.named_scope("base_sum_two"):
        second_got = traded(sends([tiles, first_got]), 1)
    with jax.named_scope("update_second"):
        new_a = (own - second_rate * summed[:mine]).astype(BF)
        order = [
            (a * n_t + b, b * n_t + a) for a in range(n_t) for b in range(n_t)
        ]
        _, second_got = lax.optimization_barrier((new_a, second_got))
        moved = lax.ppermute(new_a, ("y", "h1", "x", "zl"), order)
    with jax.named_scope("q_other"):
        q_near = summed[mine:].astype(BF)
        q_far = swap_core(q_near)
    with jax.named_scope("base_sum_three"):
        third_sends = sends([tiles, first_got, second_got])
        moved, third_sends = lax.optimization_barrier((moved, third_sends))
        third_got = traded(third_sends, 2)
        sums = totals([tiles, first_got, second_got], 2, part_of)
        sums = [v + g.astype(F32) for v, g in zip(sums, third_got)]
    with jax.named_scope("second_gather"):
        a_all = everyone(moved, T).reshape(n_t * mine, 2 * rank)
    with jax.named_scope("combine"):
        hidden = hidden_for_all(
            core, sums, a_all, q_near, q_far, cols, n_t, first_rate
        )
    with jax.named_scope("hidden_gather"):
        hidden = lax.all_to_all(hidden, T, 0, 0, tiled=True)
    with jax.named_scope("down"):
        def down(which):
            some = lax.dynamic_slice_in_dim(hidden, which * (n_t // 2), n_t // 2, 0)
            out = lax.dot_general(
                some, down_weight_base, (((1,), (0,)), ((), ())), preferred_element_type=F32
            )
            return out.reshape(rows // 2, feats)

        other = swap_core(down(1 - core).astype(BF))
        half = down(core) + other.astype(F32)
    with jax.named_scope("out_scatter"):
        pieces = half.astype(BF).reshape(n_y, rows // 2 // n_y, feats)
        landed = lax.all_to_all(pieces, "y", 0, 0, tiled=True)
        part = jnp.sum(landed.astype(F32), axis=0).astype(BF)
        pieces = part.reshape(n_z, rows // 2 // n_y // n_z, feats)
        landed = lax.all_to_all(pieces, Z, 0, 0, tiled=True)
        final = jnp.sum(landed.astype(F32), axis=0).astype(BF)
    with jax.named_scope("out_gather"):
        line = everyone(final, Z).reshape(rows // 2 // n_y, feats)
        near = everyone(line, "y").reshape(rows // 2, feats)
        far = swap_core(near)
        pair = placed(1 - core, far, placed(core, near))
        return pair.reshape(steps, step_rows, feats)


def solution(mesh):
    torus = Mesh(
        mesh.devices.reshape(4, 2, 2, 2, 4, 2), ("y", "h1", "h0", "c", "x", "zl")
    )
    return jax.shard_map(
        on_device,
        mesh=torus,
        in_specs=(
            P(DP, T),
            P(DP, T),
            P(DP, T),
            P(T, None),
            P(None, T),
            P(T, None),
            P(None, T),
            P(T, DP),
            P(T, DP),
            P(DP, T),
            P(None, None, T),
        ),
        out_specs=P(None, None, T),
        check_vma=False,
    )
```
